32 devices in a mesh: group: 2 (over x), expert: 8 (over z, y), dp: 2 (over core).
Axes of the slice: x: 2, y: 2, z: 4, core: 2. Of those that a mesh axis runs over, the one named last changes fastest.
Arguments:
- tokens: bfloat16 [8192, 1024], P(('group', 'expert', 'dp')), parts along dimension 0, may hold values from -6 to 6
- routes: int32 [8192, 2], P(('group', 'expert', 'dp')), parts along dimension 0, may hold values from 0 to 63, all different within a row; in each aligned block of 256 rows (0 to 255, 256 to 511, ...) at most 16 rows name the same one
- gate_values: float32 [8192, 2], P(('group', 'expert', 'dp')), parts along dimension 0, may hold values from 0.1 to 1
- up_weight: bfloat16 [64, 1024, 1024], P('expert'), may hold values from -0.1875 to 0.1875
- down_weight: bfloat16 [64, 1024, 1024], P('expert'), may hold values from -0.1875 to 0.1875
- grad_out: bfloat16 [8192, 1024], P(('group', 'expert', 'dp')), parts along dimension 0, may hold values from -6 to 6
Outputs:
- grad_tokens: bfloat16 [8192, 1024], P(('group', 'expert', 'dp')), parts along dimension 0
- grad_gates: float32 [8192, 2], P(('group', 'expert', 'dp')), parts along dimension 0
- grad_up: bfloat16 [128, 1024, 1024], P(('group', 'expert'), 'dp'), parts along dimension 0
- grad_down: bfloat16 [128, 1024, 1024], P(('group', 'expert'), 'dp'), parts along dimension 0
The draws below stay inside these ranges and needn't reach their ends.
There are 2 independent parts, one for each index of `group`. The reference program is written for one: setup_inputs(seed, part) draws one part's arguments, and reference() takes and returns one part's arrays. A program takes and returns all parts, laid end to end along the dimension named above; an argument that names none is the same for every part. Nothing has to cross between parts.
Inputs may be any that keep to these rules, and one draw needn't show every extreme that they name: `routes`: each token names two different experts. Among the 256 tokens of one device no expert is named more than 16 times, and in every draw some expert is named exactly 16 times by the tokens of some device.
All inputs are finite; a program needn't handle non-finite values.
Results may differ from the reference program's by a relative error of at most 0.0065.
Values may be sent and summed in bfloat16 or wider, within the bound.
No kernel may reach another device: no remote copies, remote signals or barrier semaphores. Data moves between devices by JAX's collectives and lax.ppermute only.
A program may use at most 192 MiB of HBM per device.

```python
import math
import jax
import jax.numpy as jnp
import numpy as np
from jax import lax

D = 1024
FF = 1024
EXPERTS = 64
TOK_DEV = 256
CAP = 16
TOKENS = 4096


def block_levels(key, shape, split, least, largest):
    level = 1.0
    for axis_at, parts in split:
        steps = jax.random.uniform(jax.random.fold_in(jax.random.fold_in(key, 6), axis_at), (parts,), jnp.float32, least / len(split), largest / len(split))
        level = level * jnp.repeat(jnp.exp(steps), shape[axis_at] // parts).reshape((-1,) + (1,) * (len(shape) - 1 - axis_at))
    return level


def routed_block(key, own, number, rows, count, top, reach, skew):
    order = jax.random.permutation(key, count)
    packed, ordinary = load_shares(count, rows * top, reach, skew, True), load_shares(count, rows * top, reach, skew, False)
    places = jnp.arange(count)

    def named(sizes, offset_by):
        used = int((sizes > 0).sum())
        fixed = max(1, used // 4)
        shifted = fixed + (places - fixed + offset_by * (used - fixed)) % max(1, count - fixed)
        return jnp.zeros((count,), jnp.int32).at[order[jnp.where(places < fixed, places, shifted)]].set(jnp.asarray(sizes, jnp.int32))

    sizes = jnp.where(number % 4 == 0, named(packed, number // 4), named(ordinary, number - number // 4 - 1))
    mixed = jax.random.permutation(jax.random.fold_in(own, 3), count)
    source_of, taker = mixed[0:count // 2 * 2:2], mixed[1:count // 2 * 2:2]
    margin = jnp.minimum(sizes[source_of] - 1, reach - sizes[taker]) // 2
    margin = jnp.where((source_of == order[0]) | (taker == order[0]) | (sizes[taker] == 0), 0, jnp.maximum(margin, 0))
    shifted = jax.random.randint(jax.random.fold_in(own, 4), (count // 2,), 0, 1 << 20) % (margin + 1)
    sizes = sizes.at[source_of].add(-shifted).at[taker].add(shifted)
    members = jnp.searchsorted(jnp.cumsum(sizes), jnp.arange(rows * top), side="right").astype(jnp.int32)
    table = members.reshape(top, rows).T
    table = table[jax.random.permutation(jax.random.fold_in(own, 1), rows)]
    offset_by = jax.random.randint(jax.random.fold_in(own, 2), (rows, 1), 0, top)
    return jnp.take_along_axis(table, (jnp.arange(top)[None, :] + offset_by) % top, axis=1)


def load_shares(amount, total, reach, slope, full):
    weights = [(1 << 20) // math.isqrt(rank ** slope) + 1 for rank in range(1, amount + 1)]
    largest = reach if full else min(reach, max(-(-total // amount), total * weights[0] // sum(weights)))
    least = 1 if total - largest >= amount - 1 else 0
    holding, surplus = [largest] + [least] * (amount - 1), total - largest - least * (amount - 1)
    while surplus > 0:
        movable = [i for i in range(1, amount) if holding[i] < largest] or [i for i in range(1, amount) if holding[i] < reach]
        mass, budget = sum([weights[i] for i in movable]), surplus
        for i in movable:
            addition = min(reach - holding[i], max(1, budget * weights[i] // mass), surplus)
            holding[i] = holding[i] + addition
            surplus = surplus - addition
    return np.array(holding)


def centred(stream_key, shape, width, bound, shards=(), kind=jnp.bfloat16):
    result = jax.random.normal(stream_key, shape, jnp.float32) * width
    if len(shards) > 0:
        result = block_levels(stream_key, shape, shards, -0.22, 0.18) * result
    return jnp.clip(result, min=-bound, max=bound).astype(kind)


def setup_inputs(seed: int = 0, part: int = 0) -> dict:
    key_of = jax.random.split(jax.random.key(seed), 7)
    part_splits = jax.random.split(jax.random.fold_in(key_of[6], part), 7)
    tokens = centred(part_splits[0], (TOKENS, D), 1.0, 6.0, ((0, 16),))
    routes_keys = jax.random.split(jax.random.fold_in(part_splits[1], 1), TOKENS // TOK_DEV)
    routes_turns = jax.random.permutation(jax.random.fold_in(part_splits[1], 3), TOKENS // TOK_DEV)
    routes = jax.vmap(lambda own, number: routed_block(jax.random.fold_in(part_splits[1], 2), own, number, TOK_DEV, EXPERTS, 2, CAP, 2))(routes_keys, routes_turns).reshape((TOKENS, 2))
    gate_values = jnp.clip(0.1 + 0.9 * jax.random.uniform(part_splits[2], (TOKENS, 2), jnp.float32) ** block_levels(part_splits[2], (TOKENS, 2), ((0, 16),), -0.2, 0.2), 0.1, 1.0)
    up_weight = centred(key_of[3], (EXPERTS, FF, D), D ** -0.5, 0.1875, ((0, 8),))
    down_weight = centred(key_of[4], (EXPERTS, FF, D), FF ** -0.5, 0.1875, ((0, 8),))
    grad_out = centred(part_splits[5], (TOKENS, D), 1.0, 6.0, ((0, 16),))
    return dict(tokens=tokens, routes=routes, gate_values=gate_values, up_weight=up_weight, down_weight=down_weight, grad_out=grad_out)


def slot_rows(routes):
    blocks = routes.shape[0] // TOK_DEV
    pair_ids = routes.reshape(blocks, TOK_DEV * 2)
    onehot = (pair_ids[:, :, None] == jnp.arange(EXPERTS, dtype=jnp.int32)[None, None, :]).astype(jnp.int32)
    ranking = jnp.sum(jnp.cumsum(onehot, axis=1) * onehot, axis=2) - 1
    block_ids = jnp.arange(blocks, dtype=jnp.int32)[:, None]
    target = pair_ids * (blocks * CAP) + block_ids * CAP + ranking
    return target.reshape(-1).astype(jnp.int32)


def expert_step(inputs):
    x_rows, d_rows, up_mat, down_mat = inputs
    pre_act = jnp.dot(x_rows, up_mat.T, preferred_element_type=jnp.float32)
    active = jax.nn.silu(pre_act).astype(jnp.bfloat16)
    outputs = jnp.dot(active, down_mat, preferred_element_type=jnp.float32).astype(jnp.bfloat16)
    grad_act = jnp.dot(d_rows, down_mat.T, preferred_element_type=jnp.float32)
    sigmoid_val = jax.nn.sigmoid(pre_act)
    grad_pre = (grad_act * sigmoid_val * (1.0 + pre_act * (1.0 - sigmoid_val))).astype(jnp.bfloat16)
    grad_x = jnp.dot(grad_pre, up_mat, preferred_element_type=jnp.float32).astype(jnp.bfloat16)
    grad_up = jnp.dot(grad_pre.T, x_rows, preferred_element_type=jnp.float32)
    grad_down = jnp.dot(active.T, d_rows, preferred_element_type=jnp.float32)
    return outputs, grad_x, grad_up.astype(jnp.bfloat16), grad_down.astype(jnp.bfloat16)


def reference(tokens, routes, gate_values, up_weight, down_weight, grad_out):
    blocks = tokens.shape[0] // TOK_DEV
    model_width = tokens.shape[1]
    target = slot_rows(routes)
    buffer_rows = EXPERTS * blocks * CAP
    spread = (gate_values[:, :, None] * grad_out[:, None, :].astype(jnp.float32)).astype(jnp.bfloat16)
    empty = jnp.zeros((buffer_rows, model_width), jnp.bfloat16)
    x_buffer = empty.at[target].set(jnp.repeat(tokens, 2, axis=0)).reshape(EXPERTS, blocks * CAP, model_width)
    d_buffer = empty.at[target].set(spread.reshape(-1, model_width)).reshape(EXPERTS, blocks * CAP, model_width)
    outputs, grad_x, grad_up, grad_down = lax.map(expert_step, (x_buffer, d_buffer, up_weight, down_weight))
    y_pairs = outputs.reshape(buffer_rows, model_width)[target].reshape(-1, 2, model_width)
    gx_pairs = grad_x.reshape(buffer_rows, model_width)[target].reshape(-1, 2, model_width)
    grad_gates = jnp.sum(grad_out[:, None, :].astype(jnp.float32) * y_pairs.astype(jnp.float32), axis=2)
    grad_tokens = jnp.sum(gx_pairs.astype(jnp.float32), axis=1).astype(jnp.bfloat16)
    return grad_tokens, grad_gates, grad_up, grad_down
```

```python
import functools

import jax
import jax.numpy as jnp
from jax import lax
from jax.experimental import pallas as pl
from jax.experimental.pallas import tpu as pltpu
from jax.sharding import PartitionSpec as P

EXPERTS = 64
CAP = 16
BF = jnp.bfloat16
F32 = jnp.float32
VMEM_LIMIT = 56 * 1024 * 1024
NT = (((1,), (1,)), ((), ()))
NN = (((1,), (0,)), ((), ()))
TN = (((0,), (0,)), ((), ()))


def dot(a, b, dims, precision=None):
    return lax.dot_general(a, b, dims, preferred_element_type=F32, precision=precision)


def params():
    return pltpu.CompilerParams(vmem_limit_bytes=VMEM_LIMIT)


def cost(flops, nbytes):
    return pl.CostEstimate(flops=int(flops), bytes_accessed=int(nbytes), transcendentals=0)


def targets(info):
    tokens = info.shape[1]
    first, second = info[0:1, :].astype(jnp.int32), info[1:2, :].astype(jnp.int32)
    experts = lax.broadcasted_iota(jnp.int32, (EXPERTS, tokens), 0)
    one = (experts == first).astype(F32)
    two = (experts == second).astype(F32)
    earlier = lax.broadcasted_iota(jnp.int32, (tokens, tokens), 0) < lax.broadcasted_iota(
        jnp.int32, (tokens, tokens), 1
    )
    before = dot((one + two).astype(BF), earlier.astype(F32).astype(BF), NN)
    rank_one = jnp.sum(one * before, axis=0, keepdims=True).astype(jnp.int32)
    rank_two = jnp.sum(two * (before + one), axis=0, keepdims=True).astype(jnp.int32)
    return first * CAP + rank_one, second * CAP + rank_two


def route_kernel(peers, chip_ref, info_ref, g_ref, select_ref, *d_refs):
    tokens = info_ref.shape[1]
    slots = d_refs[0].shape[0]
    info = info_ref[...]
    tgt_one, tgt_two = targets(info)
    gate_one, gate_two = info[2:3, :], info[3:4, :]
    for m in range(peers):
        rows = lax.broadcasted_iota(jnp.int32, (slots, tokens), 0) + chip_ref[m] * slots
        is_one, is_two = rows == tgt_one, rows == tgt_two
        gates = jnp.where(is_one, gate_one, 0.0) + jnp.where(is_two, gate_two, 0.0)
        gate = jnp.sum(gates, axis=1, keepdims=True)
        select = jnp.where(is_one | is_two, 1.0, 0.0).astype(BF)
        select_ref[m] = select
        d_refs[m][...] = (gate * dot(select, g_ref[...], NN)).astype(BF)


def route(chips, info, g, slots):
    peers = chips.shape[0]
    tokens, width = g.shape
    out = pl.pallas_call(
        functools.partial(route_kernel, peers),
        out_shape=[jax.ShapeDtypeStruct((peers, slots, tokens), BF)]
        + [jax.ShapeDtypeStruct((slots, width), BF)] * peers,
        in_specs=[
            pl.BlockSpec(memory_space=pltpu.SMEM),
            pl.BlockSpec(memory_space=pltpu.VMEM),
            pl.BlockSpec(memory_space=pltpu.VMEM),
        ],
        out_specs=[pl.BlockSpec(memory_space=pltpu.VMEM)] * (peers + 1),
        compiler_params=params(),
        cost_estimate=cost(2 * peers * slots * tokens * width, 4 * peers * slots * width),
        name="route",
    )(chips, info, g)
    return out[0], list(out[1:])


def pick_kernel(peers, select_ref, x_ref, *out_refs):
    for m in range(peers):
        out_refs[m][...] = dot(select_ref[m], x_ref[...], NN).astype(BF)


def pick(select, x):
    peers, slots, tokens = select.shape
    width = x.shape[1]
    return list(
        pl.pallas_call(
            functools.partial(pick_kernel, peers),
            out_shape=[jax.ShapeDtypeStruct((slots, width), BF)] * peers,
            in_specs=[pl.BlockSpec(memory_space=pltpu.VMEM)] * 2,
            out_specs=[pl.BlockSpec(memory_space=pltpu.VMEM)] * peers,
            compiler_params=params(),
            cost_estimate=cost(2 * peers * slots * tokens * width, 4 * peers * slots * width),
            name="pick",
        )(select, x)
    )


def down_kernel(count, down_ref, *refs):
    d_refs, h_ref, cat_ref = refs[:count], refs[count], refs[count + 1]
    rows = jnp.concatenate([r[...] for r in d_refs], axis=0)
    cat_ref[0] = rows
    h_ref[0] = dot(rows, down_ref[0], NT)


def down_pass(down, d_rows):
    experts, hidden, width = down.shape
    count = len(d_rows)
    rows = count * CAP
    return pl.pallas_call(
        functools.partial(down_kernel, count),
        grid=(experts,),
        out_shape=[
            jax.ShapeDtypeStruct((experts, rows, hidden), F32),
            jax.ShapeDtypeStruct((experts, rows, width), BF),
        ],
        in_specs=[pl.BlockSpec((1, hidden, width), lambda j: (j, 0, 0))]
        + [pl.BlockSpec((CAP, width), lambda j: (j, 0))] * count,
        out_specs=[
            pl.BlockSpec((1, rows, hidden), lambda j: (j, 0, 0)),
            pl.BlockSpec((1, rows, width), lambda j: (j, 0, 0)),
        ],
        compiler_params=params(),
        cost_estimate=cost(
            2 * experts * rows * hidden * width, 2 * experts * hidden * width + 8 * experts * rows * width
        ),
        name="down_pass",
    )(down, *d_rows)


def up_kernel(count, core_ref, up_ref, h_ref, *refs):
    x_refs = refs[:count]
    gx_refs = refs[count : 2 * count]
    pack_ref, mine_ref, s_ref = refs[2 * count :]
    width = x_refs[0].shape[1]
    half = mine_ref.shape[2] // 2
    rows = jnp.concatenate([r[...] for r in x_refs], axis=0)
    h = h_ref[0]
    pre = dot(rows, up_ref[0], NT)
    sig = 1.0 / (1.0 + jnp.exp(-pre))
    active = (pre * sig).astype(BF)
    grad_pre = (h * sig * (1.0 + pre * (1.0 - sig))).astype(BF)
    gx = dot(grad_pre, up_ref[0], NN).astype(BF)
    for i, ref in enumerate(gx_refs):
        ref[...] = gx[i * CAP : (i + 1) * CAP]
    prod = active.astype(F32) * h
    part = prod[:, 0:128]
    for i in range(1, prod.shape[1] // 128):
        part = part + prod[:, i * 128 : (i + 1) * 128]
    s_ref[0] = jnp.sum(part.T, axis=0, keepdims=True)
    pack_ref[0, :, 0:width] = rows

    def place(low, high):
        mine_ref[0, :, 0:half] = active[:, low : low + half]
        mine_ref[0, :, half:] = grad_pre[:, low : low + half]
        pack_ref[0, :, width : width + half] = active[:, high : high + half]
        pack_ref[0, :, width + half :] = grad_pre[:, high : high + half]

    pl.when(core_ref[0] == 0)(lambda: place(0, half))
    pl.when(core_ref[0] != 0)(lambda: place(half, 0))


def up_pass(core, up, h, x_rows):
    experts, hidden, width = up.shape
    count = len(x_rows)
    rows = count * CAP
    block = lambda *shape: pl.BlockSpec(shape, lambda j: (j,) + (0,) * (len(shape) - 1))
    out = pl.pallas_call(
        functools.partial(up_kernel, count),
        grid=(experts,),
        out_shape=[jax.ShapeDtypeStruct((experts * CAP, width), BF)] * count
        + [
            jax.ShapeDtypeStruct((experts, rows, width + hidden), BF),
            jax.ShapeDtypeStruct((experts, rows, hidden), BF),
            jax.ShapeDtypeStruct((experts, 1, rows), F32),
        ],
        in_specs=[pl.BlockSpec(memory_space=pltpu.SMEM), block(1, hidden, width), block(1, rows, hidden)]
        + [block(CAP, width)] * count,
        out_specs=[block(CAP, width)] * count
        + [block(1, rows, width + hidden), block(1, rows, hidden), block(1, 1, rows)],
        compiler_params=params(),
        cost_estimate=cost(
            4 * experts * rows * hidden * width,
            2 * experts * hidden * width + 14 * experts * rows * width,
        ),
        name="up_pass",
    )(core, up, h, *x_rows)
    return list(out[:count]), out[count], out[count + 1], out[count + 2]


def weight_kernel(width, mine_ref, pack_ref, other_ref, d_ref, d_other_ref, up_ref, down_ref):
    half = up_ref.shape[1]
    active = jnp.concatenate([mine_ref[0, :, 0:half], other_ref[0, :, width : width + half]], axis=0)
    grad_pre = jnp.concatenate([mine_ref[0, :, half:], other_ref[0, :, width + half :]], axis=0)
    x = jnp.concatenate([pack_ref[0, :, 0:width], other_ref[0, :, 0:width]], axis=0)
    d = jnp.concatenate([d_ref[0], d_other_ref[0]], axis=0)
    up_ref[0] = dot(grad_pre, x, TN).astype(BF)
    down_ref[0] = dot(active, d, TN).astype(BF)


def weight_pass(mine, pack, other, d, d_other):
    experts, rows, width = d.shape
    hidden = mine.shape[2]
    block = lambda *shape: pl.BlockSpec(shape, lambda j: (j, 0, 0))
    return pl.pallas_call(
        functools.partial(weight_kernel, width),
        grid=(experts,),
        out_shape=[jax.ShapeDtypeStruct((experts, hidden // 2, width), BF)] * 2,
        in_specs=[
            block(1, rows, hidden),
            block(1, rows, width),
            block(1, rows, width + hidden),
            block(1, rows, width),
            block(1, rows, width),
        ],
        out_specs=[block(1, hidden // 2, width)] * 2,
        compiler_params=params(),
        cost_estimate=cost(
            8 * experts * rows * hidden // 2 * width,
            2 * experts * hidden * width + 12 * experts * rows * width,
        ),
        name="weight_pass",
    )(mine, pack, other, d, d_other)


def combine_kernel(count, final, select_ref, *refs):
    total = None
    for m in range(count):
        term = dot(select_ref[m], refs[m][...], TN)
        total = term if total is None else total + term
    if final:
        total = total.astype(BF).astype(F32) + refs[count][...].astype(F32)
    refs[-1][...] = total.astype(BF)


def combine(select, rows, extra=None):
    peers, slots, tokens = select.shape
    width = rows[0].shape[1]
    final = extra is not None
    return pl.pallas_call(
        functools.partial(combine_kernel, peers, final),
        out_shape=jax.ShapeDtypeStruct((tokens, width), BF),
        in_specs=[pl.BlockSpec(memory_space=pltpu.VMEM)] * (1 + peers + final),
        out_specs=pl.BlockSpec(memory_space=pltpu.VMEM),
        compiler_params=params(),
        cost_estimate=cost(2 * peers * slots * tokens * width, 2 * peers * slots * width),
        name="combine",
    )(select, *rows, *((extra,) if final else ()))


def gates_kernel(info_ref, s_ref, out_ref):
    chips, slots = s_ref.shape
    info = info_ref[...]
    tokens = info.shape[1]
    for k, tgt in enumerate(targets(info)):
        chip = (lax.broadcasted_iota(jnp.int32, (chips, tokens), 0) == tgt // slots).astype(F32)
        row = (lax.broadcasted_iota(jnp.int32, (slots, tokens), 0) == tgt % slots).astype(F32)
        spread = dot(s_ref[...], chip, TN, lax.Precision.HIGHEST)
        value = jnp.sum(row * spread, axis=0, keepdims=True)
        out_ref[k : k + 1, :] = value / info[2 + k : 3 + k, :]


def gates_pass(info, s):
    return pl.pallas_call(
        gates_kernel,
        out_shape=jax.ShapeDtypeStruct((2, info.shape[1]), F32),
        in_specs=[pl.BlockSpec(memory_space=pltpu.VMEM)] * 2,
        out_specs=pl.BlockSpec(memory_space=pltpu.VMEM),
        compiler_params=params(),
        cost_estimate=cost(1 << 20, 1 << 16),
        name="gates",
    )(info, s)


def per_device(tokens, routes, gate_values, up_weight, down_weight, grad_out):
    chips = lax.axis_size("expert")
    half = chips // 2
    local_experts = up_weight.shape[0]
    slots = local_experts * CAP
    me = lax.axis_index("expert").astype(jnp.int32)
    core = lax.axis_index("dp").astype(jnp.int32).reshape(1)
    near = me ^ jnp.arange(half, dtype=jnp.int32)

    def swap(value, m):
        return lax.ppermute(value, "expert", [(i, i ^ m) for i in range(chips)])

    def swap_core(value):
        return lax.ppermute(value, "dp", [(0, 1), (1, 0)])

    def deal(rows):
        return [rows[0]] + [swap(rows[m], m) for m in range(1, half)]

    info = jnp.concatenate(
        [routes.T.astype(F32), gate_values.T, jnp.zeros((4, tokens.shape[0]), F32)], axis=0
    )
    info_far = swap(info, half)
    g_far = swap(grad_out, half)
    x_far = swap(tokens, half)

    select, d_near = route(near, info, grad_out, slots)
    d_rows = deal(d_near)
    x_rows = deal(pick(select, tokens))
    select_far, d_deal = route(near, info_far, g_far, slots)
    d_rows = d_rows + deal(d_deal)
    x_rows = x_rows + deal(pick(select_far, x_far))

    h, d_cat = down_pass(down_weight, d_rows)
    d_other = swap_core(d_cat)
    gx, pack, mine, s = up_pass(core, up_weight, h, x_rows)

    gx_far = combine(select_far, deal(gx[half:]))
    gx_back = swap(gx_far, half)
    gx_near = deal(gx[:half])

    s_near = s.reshape(local_experts, chips, CAP).transpose(1, 0, 2).reshape(chips, slots)
    s_near = jnp.take(s_near, jnp.arange(chips, dtype=jnp.int32) ^ me, axis=0)
    s_back = lax.all_to_all(s_near, "expert", split_axis=0, concat_axis=0, tiled=True)
    grad_gates = gates_pass(info, s_back).T

    grad_up, grad_down = weight_pass(mine, pack, swap_core(pack), d_cat, d_other)
    grad_tokens = combine(select, gx_near, gx_back)
    return grad_tokens, grad_gates, grad_up, grad_down


def solution(mesh):
    placed = (
        P(("group", "expert", "dp"), None),
        P(("group", "expert", "dp"), None),
        P(("group", "expert", "dp"), None),
        P("expert", None, None),
        P("expert", None, None),
        P(("group", "expert", "dp"), None),
    )
    return jax.shard_map(
        per_device,
        mesh=mesh,
        in_specs=placed,
        out_specs=(
            P(("group", "expert", "dp"), None),
            P(("group", "expert", "dp"), None),
            P(("group", "expert"), "dp", None),
            P(("group", "expert"), "dp", None),
        ),
        check_vma=False,
    )
```

```python
import functools

import jax
import jax.numpy as jnp
from jax import lax
from jax.experimental import pallas as pl
from jax.experimental.pallas import tpu as pltpu
from jax.sharding import PartitionSpec as P

EXPERTS = 64
CAP = 16
BF = jnp.bfloat16
F32 = jnp.float32
NT = (((1,), (1,)), ((), ()))
NN = (((1,), (0,)), ((), ()))
TN = (((0,), (0,)), ((), ()))


def dot(a, b, dims, precision=None):
    return lax.dot_general(a, b, dims, preferred_element_type=F32, precision=precision)


COST = pl.CostEstimate(flops=1 << 20, bytes_accessed=1 << 20, transcendentals=0)


def params(mebibytes=14):
    return pltpu.CompilerParams(vmem_limit_bytes=mebibytes * 1024 * 1024)


def targets(routes):
    tokens = routes.shape[1]
    first, second = routes[0:1, :], routes[1:2, :]
    experts = lax.broadcasted_iota(jnp.int32, (EXPERTS, tokens), 0)
    one = (experts == first).astype(F32)
    two = (experts == second).astype(F32)
    earlier = lax.broadcasted_iota(jnp.int32, (tokens, tokens), 0) < lax.broadcasted_iota(
        jnp.int32, (tokens, tokens), 1
    )
    before = dot((one + two).astype(BF), earlier.astype(F32).astype(BF), NN)
    rank_one = jnp.sum(one * before, axis=0, keepdims=True).astype(jnp.int32)
    rank_two = jnp.sum(two * (before + one), axis=0, keepdims=True).astype(jnp.int32)
    return first * CAP + rank_one, second * CAP + rank_two


def thirds(value):
    high = value.astype(BF)
    rest = value - high.astype(F32)
    mid = rest.astype(BF)
    return [high, mid, (rest - mid.astype(F32)).astype(BF)]


def added(rows):
    rows = rows.astype(F32)
    return rows[0:1, :] + rows[1:2, :] + rows[2:3, :]


def prepare_kernel(routes_ref, gates_ref, g_hbm, out_ref, sem):
    tokens, width = g_hbm.shape
    copy = pltpu.make_async_copy(g_hbm, out_ref.at[0:tokens], sem)
    copy.start()
    routes = routes_ref[...].astype(F32).astype(BF)
    gates = gates_ref[...]
    rows = [routes, *thirds(gates[0:1, :]), *thirds(gates[1:2, :]), jnp.zeros((CAP - 8, tokens), BF)]
    out_ref[tokens:, 0:tokens] = jnp.concatenate(rows, axis=0)
    out_ref[tokens:, tokens:] = jnp.zeros((CAP, width - tokens), BF)
    copy.wait()


def prepare(routes, gates, g):
    tokens, width = g.shape
    return pl.pallas_call(
        prepare_kernel,
        out_shape=jax.ShapeDtypeStruct((tokens + CAP, width), BF),
        in_specs=[pl.BlockSpec(memory_space=pltpu.VMEM)] * 2 + [pl.BlockSpec(memory_space=pl.ANY)],
        out_specs=pl.BlockSpec(memory_space=pltpu.VMEM),
        scratch_shapes=[pltpu.SemaphoreType.DMA],
        compiler_params=params(),
        cost_estimate=COST,
        name="prepare",
    )(routes, gates, g)


def facts_of(g_ref, tokens):
    facts = g_ref[tokens : tokens + 8, 0:tokens]
    return targets(facts[0:2, :].astype(F32).astype(jnp.int32)), (added(facts[2:5, :]), added(facts[5:8, :]))


def select_slots(targets_of, gates, base, slots):
    rows = lax.broadcasted_iota(jnp.int32, (slots, targets_of[0].shape[1]), 0) + base
    is_one, is_two = rows == targets_of[0], rows == targets_of[1]
    gate = jnp.where(is_one, gates[0], 0.0) + jnp.where(is_two, gates[1], 0.0)
    return jnp.where(is_one | is_two, 1.0, 0.0).astype(BF), jnp.sum(gate, axis=1, keepdims=True)


def whole(*shape):
    return pl.BlockSpec(shape, lambda j: (0,) * len(shape), pipeline_mode=pl.Buffered(1))


def by_expert(*shape):
    return pl.BlockSpec(shape, lambda j: (j,) + (0,) * (len(shape) - 1))


def d_kernel(peers, me_ref, g_ref, select_ref, facts_ref, *d_refs):
    slots, tokens = select_ref.shape[1:]
    tgt, gates = facts_of(g_ref, tokens)
    for m in range(peers):
        select, gate = select_slots(tgt, gates, (me_ref[0] ^ m) * slots, slots)
        select_ref[m] = select
        d_refs[m][...] = (gate * dot(select, g_ref[0:tokens], NN)).astype(BF)
    facts_ref[0:2] = jnp.concatenate(tgt, axis=0).astype(F32)
    facts_ref[2:4] = jnp.concatenate(gates, axis=0)
    facts_ref[4:8] = jnp.zeros((4, tokens), F32)


SCALARS = pl.BlockSpec(memory_space=pltpu.SMEM)
VECTORS = pl.BlockSpec(memory_space=pltpu.VMEM)


def d_pass(name, me, g, peers, slots):
    tokens, width = g.shape[0] - CAP, g.shape[1]
    out = pl.pallas_call(
        functools.partial(d_kernel, peers),
        out_shape=[jax.ShapeDtypeStruct((peers, slots, tokens), BF), jax.ShapeDtypeStruct((8, tokens), F32)]
        + [jax.ShapeDtypeStruct((slots, width), BF)] * peers,
        in_specs=[SCALARS, VECTORS],
        out_specs=[VECTORS] * (2 + peers),
        compiler_params=params(),
        cost_estimate=COST,
        name=name,
    )(me, g)
    return out[0], out[1], list(out[2:])


def x_kernel(peers, near_ref, x_near_ref, far_ref, x_far_ref, *out_refs):
    slots = near_ref.shape[1]
    for m in range(peers):
        out_refs[m][0:slots] = dot(near_ref[m], x_near_ref[...], NN).astype(BF)
        out_refs[m][slots:] = dot(far_ref[m], x_far_ref[...], NN).astype(BF)


def x_pass(select_near, x_near, select_far, x_far):
    peers, slots, _ = select_near.shape
    return list(
        pl.pallas_call(
            functools.partial(x_kernel, peers),
            out_shape=[jax.ShapeDtypeStruct((2 * slots, x_near.shape[1]), BF)] * peers,
            in_specs=[VECTORS] * 4,
            out_specs=[VECTORS] * peers,
            compiler_params=params(),
            cost_estimate=COST,
            name="x_rows",
        )(select_near, x_near, select_far, x_far)
    )


IN_HBM = pl.BlockSpec(memory_space=pltpu.HBM)


def in_hbm(value):
    return pltpu.with_memory_space_constraint(value, pltpu.HBM)


def fetch(weight_hbm, weight_ref, sem):
    copies = [
        pltpu.make_async_copy(weight_hbm.at[j], weight_ref.at[j], sem.at[j]) for j in range(weight_hbm.shape[0])
    ]
    for copy in copies:
        copy.start()
    return copies


def joined(parts):
    return jnp.concatenate(parts, axis=0)


def of_expert(j, first=0):
    return slice(first + j * CAP, first + (j + 1) * CAP)


def expert_rows(j, refs, first=0):
    return [ref[first + j * CAP : first + (j + 1) * CAP] for ref in refs]


def down_kernel(peers, weight_hbm, *refs):
    d_refs, (h_ref, d_ref, weight_ref, sem) = refs[: 2 * peers], refs[2 * peers :]
    for j, copy in enumerate(fetch(weight_hbm, weight_ref, sem)):
        rows = joined(expert_rows(j, d_refs))
        d_ref[j] = rows
        copy.wait()
        h_ref[j] = dot(rows, weight_ref[j], NT)


def down_pass(weight, near_d, far_d):
    experts, hidden, width = weight.shape
    peers = len(near_d)
    rows = 2 * peers * CAP
    return pl.pallas_call(
        functools.partial(down_kernel, peers),
        out_shape=[
            jax.ShapeDtypeStruct((experts, rows, hidden), F32),
            jax.ShapeDtypeStruct((experts, rows, width), BF),
        ],
        in_specs=[IN_HBM] + [VECTORS] * (2 * peers),
        out_specs=[VECTORS] * 2,
        scratch_shapes=[pltpu.VMEM(weight.shape, BF), pltpu.SemaphoreType.DMA((experts,))],
        compiler_params=params(24),
        cost_estimate=COST,
        name="down_pass",
    )(in_hbm(weight), *near_d, *far_d)


def up_kernel(peers, core_ref, weight_hbm, h_ref, *refs):
    groups, refs = [refs[i * peers : (i + 1) * peers] for i in range(4)], refs[4 * peers :]
    x_refs, near_gx_refs, one_refs, two_refs = groups
    pack_hbm, mine_hbm, weight_ref, part_ref, pack_ref, mine_ref, in_sem, out_sem = refs
    experts = weight_ref.shape[0]
    width, cols = x_refs[0].shape[1], one_refs[0].shape[1]
    slots, half = experts * CAP, mine_ref.shape[2] // 2
    core = core_ref[0]

    def store(j):
        return (
            pltpu.make_async_copy(pack_ref.at[j], pack_hbm.at[j], out_sem.at[j, 0]),
            pltpu.make_async_copy(mine_ref.at[j], mine_hbm.at[j], out_sem.at[j, 1]),
        )

    copies = fetch(weight_hbm, weight_ref, in_sem)

    def before(j):
        copies[j].wait()
        x = joined(expert_rows(j, x_refs) + expert_rows(j, x_refs, slots))
        pack_ref[j, :, 0:width] = x
        return dot(x, weight_ref[j], NT)

    following = before(0)
    for j in range(experts):
        at = of_expert(j)
        pre, h = following, h_ref[j]
        following = before(j + 1) if j + 1 < experts else None
        sig = 1.0 / (1.0 + jnp.exp(-pre))
        active = (pre * sig).astype(BF)
        grad_pre = (h * sig * (1.0 + pre * (1.0 - sig))).astype(BF)
        gx = dot(grad_pre, weight_ref[j], NN).astype(BF)
        prod = active.astype(F32) * h
        part = prod[:, 0:128]
        for i in range(1, prod.shape[1] // 128):
            part = part + prod[:, i * 128 : (i + 1) * 128]
        for m in range(peers):
            near, far = of_expert(m), of_expert(peers + m)
            part_ref[m, at], part_ref[peers + m, at] = part[near], part[far]
            near_gx_refs[m][at] = gx[near]
            one_refs[m][at] = gx[far, 0:cols]
            two_refs[m][at] = gx[far, cols:]
        for i, value in enumerate((active, grad_pre)):
            low, high = value[:, 0:half], value[:, half:]
            to = i * half
            mine_ref[j, :, to : to + half] = jnp.where(core == 0, low, high)
            pack_ref[j, :, width + to : width + to + half] = jnp.where(core == 0, high, low)
        for out in store(j):
            out.start()
    for m, ref in enumerate((*near_gx_refs, *one_refs)):
        total = jnp.sum(part_ref[m].T, axis=0, keepdims=True)
        ref[slots : slots + CAP, 0:slots] = joined([*thirds(total), jnp.zeros((CAP - 3, slots), BF)])
        ref[slots : slots + CAP, slots:] = jnp.zeros((CAP, ref.shape[1] - slots), BF)
    for j in range(experts):
        for out in store(j):
            out.wait()


def up_pass(core, weight, h, x):
    experts, hidden, width = weight.shape
    peers = len(x)
    count, slots, cols = 2 * peers * CAP, experts * CAP, width // 2
    pack = (experts, count, width + hidden)
    mine = (experts, count, hidden)
    shapes = [(slots + CAP, width)] * peers + [(slots + CAP, cols)] * peers + [(slots, cols)] * peers
    out = pl.pallas_call(
        functools.partial(up_kernel, peers),
        out_shape=[jax.ShapeDtypeStruct(shape, BF) for shape in (*shapes, pack, mine)],
        in_specs=[SCALARS, IN_HBM] + [VECTORS] * (1 + peers),
        out_specs=[VECTORS] * (3 * peers) + [pl.BlockSpec(memory_space=pl.ANY)] * 2,
        scratch_shapes=[
            pltpu.VMEM(weight.shape, BF),
            pltpu.VMEM((2 * peers, slots, 128), F32),
            pltpu.VMEM(pack, BF),
            pltpu.VMEM(mine, BF),
            pltpu.SemaphoreType.DMA((experts,)),
            pltpu.SemaphoreType.DMA((experts, 2)),
        ],
        compiler_params=params(28),
        cost_estimate=COST,
        name="up_pass",
    )(core, in_hbm(weight), h, *x)
    return *(list(out[i * peers : (i + 1) * peers]) for i in range(3)), out[-2], out[-1]


def weight_kernel(mine_ref, pack_ref, other_ref, d_ref, d_other_ref, up_ref, down_ref):
    half, width = up_ref.shape[1:]
    active = joined([mine_ref[0, :, 0:half], other_ref[0, :, width : width + half]])
    grad_pre = joined([mine_ref[0, :, half:], other_ref[0, :, width + half :]])
    up_ref[0] = dot(grad_pre, joined([pack_ref[0], other_ref[0, :, 0:width]]), TN).astype(BF)
    down_ref[0] = dot(active, joined([d_ref[0], d_other_ref[0]]), TN).astype(BF)


def weight_pass(mine, pack, other, d, d_other):
    experts, rows, width = d.shape
    hidden = mine.shape[2]
    return pl.pallas_call(
        weight_kernel,
        grid=(experts,),
        out_shape=[jax.ShapeDtypeStruct((experts, hidden // 2, width), BF)] * 2,
        in_specs=[by_expert(1, rows, n) for n in (hidden, width, width + hidden, width, width)],
        out_specs=[by_expert(1, hidden // 2, width)] * 2,
        compiler_params=params(),
        cost_estimate=COST,
        name="weight_pass",
    )(mine, pack, other, d, d_other)


def relay_kernel(peers, select_ref, *refs):
    out_ref = refs[peers]
    slots, tokens = select_ref.shape[1:]
    total = None
    for m in range(peers):
        term = dot(select_ref[m], refs[m][0:slots], TN)
        total = term if total is None else total + term
    out_ref[0:tokens] = total.astype(BF)
    if refs[0].shape[0] > slots:
        for m in range(peers):
            out_ref[tokens + m * CAP : tokens + (m + 1) * CAP] = refs[m][slots:]


def relay_pass(select, rows):
    peers, slots, tokens = select.shape
    width = rows[0].shape[1]
    out_rows = tokens + peers * (rows[0].shape[0] - slots)
    return pl.pallas_call(
        functools.partial(relay_kernel, peers),
        out_shape=jax.ShapeDtypeStruct((out_rows, width), BF),
        in_specs=[VECTORS] * (1 + peers),
        out_specs=VECTORS,
        compiler_params=params(),
        cost_estimate=COST,
        name="relay_sum",
    )(select, *rows)


def last_kernel(me_ref, facts_ref, select_ref, one_ref, two_ref, *refs):
    near_refs, (out_ref, gates_ref) = refs[:-2], refs[-2:]
    peers, slots, tokens = select_ref.shape
    cols = one_ref.shape[1]
    me = me_ref[0]
    tgt = facts_ref[0:1, :].astype(jnp.int32), facts_ref[1:2, :].astype(jnp.int32)
    total = None
    values = [jnp.zeros((1, tokens), F32)] * 2
    for m in range(peers):
        term = dot(select_ref[m], near_refs[m][0:slots], TN)
        total = term if total is None else total + term
        far = one_ref[tokens + m * CAP : tokens + (m + 1) * CAP, 0:slots]
        near = near_refs[m][slots : slots + CAP, 0:slots]
        for chip, tail in ((me ^ m, near), (me ^ (peers + m), far)):
            column = added(tail).T
            at = lax.broadcasted_iota(jnp.int32, (slots, tokens), 0) + chip * slots
            for k in range(2):
                hit = jnp.where(at == tgt[k], column, 0.0)
                values[k] = values[k] + jnp.sum(hit, axis=0, keepdims=True)
    gates_ref[0:1] = values[0] / facts_ref[2:3, :]
    gates_ref[1:2] = values[1] / facts_ref[3:4, :]
    total = total.astype(BF).astype(F32)
    out_ref[:, 0:cols] = (total[:, 0:cols] + one_ref[0:tokens].astype(F32)).astype(BF)
    out_ref[:, cols:] = (total[:, cols:] + two_ref[...].astype(F32)).astype(BF)


def last_pass(me, facts, select, near, one, two):
    tokens = select.shape[2]
    width = one.shape[1] + two.shape[1]
    return pl.pallas_call(
        last_kernel,
        out_shape=[jax.ShapeDtypeStruct((tokens, width), BF), jax.ShapeDtypeStruct((2, tokens), F32)],
        in_specs=[SCALARS] + [VECTORS] * (4 + len(near)),
        out_specs=[VECTORS] * 2,
        compiler_params=params(),
        cost_estimate=COST,
        name="last_sum",
    )(me, facts, select, one, two, *near)


def after(value, *others):
    return lax.optimization_barrier((value, *others))[0]


def per_device(tokens, routes, gate_values, up_weight, down_weight, grad_out):
    chips = lax.axis_size("expert")
    half = chips // 2
    slots = up_weight.shape[0] * CAP
    me = lax.axis_index("expert").astype(jnp.int32).reshape(1)
    core = lax.axis_index("dp").astype(jnp.int32).reshape(1)

    def swap(value, m):
        return lax.ppermute(value, "expert", [(i, i ^ m) for i in range(chips)])

    def swap_core(value):
        return lax.ppermute(value, "dp", [(0, 1), (1, 0)])

    def deal(rows):
        return [rows[0]] + [swap(rows[m], m) for m in range(1, half)]

    g_near = prepare(routes.T, gate_values.T, grad_out)
    g_far = swap(g_near, half)
    select, facts, near_d = d_pass("near_d_rows", me, g_near, half, slots)
    near_d = deal(near_d)
    x_far = swap(after(tokens, g_far, near_d), half)

    select_far, _, far_d = d_pass("far_d_rows", me, g_far, half, slots)
    far_d = deal(far_d)
    x = x_pass(select, tokens, select_far, after(x_far, far_d))
    h, d = down_pass(down_weight, near_d, after(far_d, x[0]))
    d_other = swap_core(d)
    gx_near, gx_one, gx_two, pack, mine = up_pass(core, up_weight, h, deal(x))
    gx_one, gx_two = deal(gx_one), deal(gx_two)
    other = swap_core(pack)

    relay_one = relay_pass(select_far, after(gx_one, d_other))
    back_one = swap(relay_one, half)
    relay_two = relay_pass(select_far, after(gx_two, other))
    back_two = swap(relay_two, half)
    gx_near = deal(after(gx_near, relay_two))

    grad_up, grad_down = weight_pass(after(mine, relay_two), pack, other, d, d_other)
    grad_tokens, grad_gates = last_pass(me, after(facts, grad_up), select, gx_near, back_one, back_two)
    return grad_tokens, grad_gates.T, grad_up, grad_down


def solution(mesh):
    placed = (
        P(("group", "expert", "dp"), None),
        P(("group", "expert", "dp"), None),
        P(("group", "expert", "dp"), None),
        P("expert", None, None),
        P("expert", None, None),
        P(("group", "expert", "dp"), None),
    )
    return jax.shard_map(
        per_device,
        mesh=mesh,
        in_specs=placed,
        out_specs=(
            P(("group", "expert", "dp"), None),
            P(("group", "expert", "dp"), None),
            P(("group", "expert"), "dp", None),
            P(("group", "expert"), "dp", None),
        ),
        check_vma=False,
    )
```

```python
import functools

import jax
import jax.numpy as jnp
from jax import lax
from jax.experimental import pallas as pl
from jax.experimental.pallas import tpu as pltpu
from jax.sharding import PartitionSpec as P

EXPERTS = 64
CAP = 16
BF = jnp.bfloat16
F32 = jnp.float32
NT = (((1,), (1,)), ((), ()))
NN = (((1,), (0,)), ((), ()))
TN = (((0,), (0,)), ((), ()))


def dot(a, b, dims, precision=None):
    return lax.dot_general(a, b, dims, preferred_element_type=F32, precision=precision)


COST = pl.CostEstimate(flops=1 << 20, bytes_accessed=1 << 20, transcendentals=0)


def params(mebibytes=14):
    return pltpu.CompilerParams(vmem_limit_bytes=mebibytes * 1024 * 1024)


def targets(routes):
    tokens = routes.shape[1]
    first, second = routes[0:1, :], routes[1:2, :]
    experts = lax.broadcasted_iota(jnp.int32, (EXPERTS, tokens), 0)
    one = (experts == first).astype(F32)
    two = (experts == second).astype(F32)
    earlier = lax.broadcasted_iota(jnp.int32, (tokens, tokens), 0) < lax.broadcasted_iota(
        jnp.int32, (tokens, tokens), 1
    )
    before = dot((one + two).astype(BF), earlier.astype(F32).astype(BF), NN)
    rank_one = jnp.sum(one * before, axis=0, keepdims=True).astype(jnp.int32)
    rank_two = jnp.sum(two * (before + one), axis=0, keepdims=True).astype(jnp.int32)
    return first * CAP + rank_one, second * CAP + rank_two


def thirds(value):
    high = value.astype(BF)
    rest = value - high.astype(F32)
    mid = rest.astype(BF)
    return [high, mid, (rest - mid.astype(F32)).astype(BF)]


def added(rows):
    rows = rows.astype(F32)
    return rows[0:1, :] + rows[1:2, :] + rows[2:3, :]


IN_HBM = pl.BlockSpec(memory_space=pltpu.HBM)


def in_hbm(value):
    return pltpu.with_memory_space_constraint(value, pltpu.HBM)


def prepare_kernel(routes_hbm, gates_hbm, g_hbm, x_hbm, out_ref, x_ref, routes_ref, gates_ref, sem):
    tokens, width = g_hbm.shape
    copies = [
        pltpu.make_async_copy(routes_hbm, routes_ref, sem.at[0]),
        pltpu.make_async_copy(gates_hbm, gates_ref, sem.at[1]),
        pltpu.make_async_copy(g_hbm, out_ref.at[0:tokens], sem.at[2]),
        pltpu.make_async_copy(x_hbm, x_ref, sem.at[3]),
    ]
    for copy in copies:
        copy.start()
    out_ref[tokens:, tokens:] = jnp.zeros((CAP, width - tokens), BF)
    copies[0].wait()
    copies[1].wait()
    routes = routes_ref[...].astype(F32).astype(BF)
    gates = gates_ref[...]
    rows = [routes, *thirds(gates[0:1, :]), *thirds(gates[1:2, :]), jnp.zeros((CAP - 8, tokens), BF)]
    out_ref[tokens:, 0:tokens] = jnp.concatenate(rows, axis=0)
    copies[2].wait()
    copies[3].wait()


def prepare(routes, gates, g, x):
    tokens, width = g.shape
    return pl.pallas_call(
        prepare_kernel,
        out_shape=[jax.ShapeDtypeStruct((tokens + CAP, width), BF), jax.ShapeDtypeStruct(x.shape, BF)],
        in_specs=[IN_HBM] * 4,
        out_specs=[pl.BlockSpec(memory_space=pltpu.VMEM)] * 2,
        scratch_shapes=[
            pltpu.VMEM(routes.shape, jnp.int32),
            pltpu.VMEM(gates.shape, F32),
            pltpu.SemaphoreType.DMA((4,)),
        ],
        compiler_params=params(),
        cost_estimate=COST,
        name="prepare",
    )(in_hbm(routes), in_hbm(gates), in_hbm(g), in_hbm(x))


def facts_of(g_ref, tokens):
    facts = g_ref[tokens : tokens + 8, 0:tokens]
    return targets(facts[0:2, :].astype(F32).astype(jnp.int32)), (added(facts[2:5, :]), added(facts[5:8, :]))


def select_slots(targets_of, gates, base, slots):
    rows = lax.broadcasted_iota(jnp.int32, (slots, targets_of[0].shape[1]), 0) + base
    is_one, is_two = rows == targets_of[0], rows == targets_of[1]
    gate = jnp.where(is_one, gates[0], 0.0) + jnp.where(is_two, gates[1], 0.0)
    return jnp.where(is_one | is_two, 1.0, 0.0).astype(BF), jnp.sum(gate, axis=1, keepdims=True)


def whole(*shape):
    return pl.BlockSpec(shape, lambda j: (0,) * len(shape), pipeline_mode=pl.Buffered(1))


def by_expert(*shape):
    return pl.BlockSpec(shape, lambda j: (j,) + (0,) * (len(shape) - 1))


def rows_kernel(peers, parts, me_ref, g_ref, x_ref, select_ref, facts_ref, *rows_refs):
    slots, tokens = select_ref.shape[1:]
    size = slots // parts
    tgt, gates = facts_of(g_ref, tokens)
    for m in range(peers):
        select, gate = select_slots(tgt, gates, (me_ref[0] ^ m) * slots, slots)
        select_ref[m] = select
        x = dot(select, x_ref[...], NN).astype(BF)
        d = (gate * dot(select, g_ref[0:tokens], NN)).astype(BF)
        for i in range(parts):
            rows_refs[i * peers + m][0:size] = x[i * size : (i + 1) * size]
            rows_refs[i * peers + m][size:] = d[i * size : (i + 1) * size]
    facts_ref[0:2] = jnp.concatenate(tgt, axis=0).astype(F32)
    facts_ref[2:4] = jnp.concatenate(gates, axis=0)
    facts_ref[4:8] = jnp.zeros((4, tokens), F32)


SCALARS = pl.BlockSpec(memory_space=pltpu.SMEM)
VECTORS = pl.BlockSpec(memory_space=pltpu.VMEM)


def rows_pass(name, parts, me, g, x, peers, slots):
    tokens, width = x.shape
    out = pl.pallas_call(
        functools.partial(rows_kernel, peers, parts),
        out_shape=[jax.ShapeDtypeStruct((peers, slots, tokens), BF), jax.ShapeDtypeStruct((8, tokens), F32)]
        + [jax.ShapeDtypeStruct((2 * slots // parts, width), BF)] * (parts * peers),
        in_specs=[SCALARS] + [VECTORS] * 2,
        out_specs=[VECTORS] * (2 + parts * peers),
        compiler_params=params(),
        cost_estimate=COST,
        name=name,
    )(me, g, x)
    return out[0], out[1], *(list(out[2 + i * peers : 2 + (i + 1) * peers]) for i in range(parts))


def fetch(weight_hbm, weight_ref, sem, first=0):
    copies = [
        pltpu.make_async_copy(weight_hbm.at[first + j], weight_ref.at[j], sem.at[j])
        for j in range(weight_ref.shape[0])
    ]
    for copy in copies:
        copy.start()
    return copies


def turn_kernel(weight_ref, out_ref):
    out_ref[0] = weight_ref[0].T


def turned(weight):
    experts, hidden, width = weight.shape
    return pl.pallas_call(
        turn_kernel,
        grid=(experts,),
        out_shape=pltpu.HBM((experts, width, hidden), weight.dtype),
        in_specs=[by_expert(1, hidden, width)],
        out_specs=by_expert(1, width, hidden),
        compiler_params=params(),
        cost_estimate=COST,
        name="turned",
    )(in_hbm(weight))


def joined(parts):
    return jnp.concatenate(parts, axis=0)


def of_expert(j, first=0):
    return slice(first + j * CAP, first + (j + 1) * CAP)


def block_kernel(peers, which, core_ref, up_hbm, down_hbm, *refs):
    def take(n):
        nonlocal refs
        taken, refs = refs[:n], refs[n:]
        return taken

    near_refs, far_refs = take(peers), take(peers)
    early_part, _ = (take(1), take(2)) if which else ((), ())
    gx_refs, part_out = take((1 + which) * peers), take(1 - which)
    pack_hbm, mine_hbm, up_ref, down_ref = take(4)
    part_ref = take(1)[0] if which else part_out[0]
    pack_ref, mine_ref, in_sem, out_sem = refs
    experts = up_ref.shape[0]
    width = far_refs[0].shape[1]
    slots, half, count = experts * CAP, mine_ref.shape[2] // 2, 2 * peers * CAP
    core = core_ref[0]

    def store(j):
        return (
            pltpu.make_async_copy(pack_ref.at[j], pack_hbm.at[which * experts + j], out_sem.at[j, 0]),
            pltpu.make_async_copy(mine_ref.at[j], mine_hbm.at[which * experts + j], out_sem.at[j, 1]),
        )

    def rows_of(j, kind):
        near, far = (2 * kind + which) * slots + j * CAP, kind * slots + j * CAP
        return joined([ref[near : near + CAP] for ref in near_refs] + [ref[far : far + CAP] for ref in far_refs])

    weights = ((up_hbm, up_ref), (down_hbm, down_ref))
    copies = [
        [
            pltpu.make_async_copy(hbm.at[which * experts + j], ref.at[j], in_sem.at[j, i])
            for i, (hbm, ref) in enumerate(weights)
        ]
        for j in range(experts)
    ]
    for group in copies:
        for copy in group:
            copy.start()

    def before(j):
        copies[j][0].wait()
        copies[j][1].wait()
        x, d = rows_of(j, 0), rows_of(j, 1)
        pack_ref[j, :, 0:width] = x
        pack_ref[j, :, width : 2 * width] = d
        return dot(x, up_ref[j], NN), dot(d, down_ref[j], NN)

    following = before(0)
    for j in range(experts):
        pre, h = following
        following = before(j + 1) if j + 1 < experts else None
        sig = 1.0 / (1.0 + jnp.exp(-pre))
        active = (pre * sig).astype(BF)
        grad_pre = (h * sig * (1.0 + pre * (1.0 - sig))).astype(BF)
        gx = dot(grad_pre, up_ref[j], NT).astype(BF)
        prod = active.astype(F32) * h
        part = prod[:, 0:128]
        for i in range(1, prod.shape[1] // 128):
            part = part + prod[:, i * 128 : (i + 1) * 128]
        for m in range(2 * peers):
            mine, to = slice(m * CAP, (m + 1) * CAP), j * CAP
            part_ref[m, to : to + CAP] = part[mine]
            if which:
                gx_refs[m][to : to + CAP] = gx[mine]
            else:
                to = to + m // peers * slots
                gx_refs[m % peers][to : to + CAP] = gx[mine]
        for i, value in enumerate((active, grad_pre)):
            low, high = value[:, 0:half], value[:, half:]
            to = i * half
            mine_ref[j, :, to : to + half] = jnp.where(core == 0, low, high)
            pack_ref[j, :, 2 * width + to : 2 * width + to + half] = jnp.where(core == 0, high, low)
        for out in store(j):
            out.start()
    if which:
        for m in range(2 * peers):
            total = jnp.sum(joined([early_part[0][m], part_ref[m]]).T, axis=0, keepdims=True)
            gx_refs[m][slots:, 0 : 2 * slots] = joined([*thirds(total), jnp.zeros((CAP - 3, 2 * slots), BF)])
            gx_refs[m][slots:, 2 * slots :] = jnp.zeros((CAP, width - 2 * slots), BF)
    for j in range(experts):
        for out in store(j):
            out.wait()


def block_pass(which, core, up, down, near, far, early=()):
    experts, width, hidden = up.shape[0] // 2, *up.shape[1:]
    peers = len(near)
    count, slots = 2 * peers * CAP, experts * CAP
    pack, mine, part = (experts, count, 2 * width + hidden), (experts, count, hidden), (2 * peers, slots, 128)
    gx = [(slots + CAP, width)] * (2 * peers) if which else [(2 * slots, width)] * peers
    anywhere = pl.BlockSpec(memory_space=pl.ANY)
    out = pl.pallas_call(
        functools.partial(block_kernel, peers, which),
        out_shape=[jax.ShapeDtypeStruct(shape, BF) for shape in gx]
        + ([] if which else [jax.ShapeDtypeStruct(part, F32)])
        + [jax.ShapeDtypeStruct((2 * experts, *shape[1:]), BF) for shape in (pack, mine)],
        in_specs=[SCALARS] + [IN_HBM] * 2 + [VECTORS] * (2 * peers + which) + [anywhere] * (2 * which),
        out_specs=[VECTORS] * (len(gx) + 1 - which) + [anywhere] * 2,
        scratch_shapes=[pltpu.VMEM((experts, width, hidden), BF)] * 2
        + [pltpu.VMEM(part, F32)] * which
        + [
            pltpu.VMEM(pack, BF),
            pltpu.VMEM(mine, BF),
            pltpu.SemaphoreType.DMA((experts, 2)),
            pltpu.SemaphoreType.DMA((experts, 2)),
        ],
        input_output_aliases={4 + 2 * peers + i: len(gx) + i for i in range(2 * which)},
        compiler_params=params(26),
        cost_estimate=COST,
        name=("first_experts", "last_experts")[which],
    )(core, in_hbm(up), in_hbm(down), *near, *far, *early)
    return list(out[: len(gx)]), *out[len(gx) :]


def weight_kernel(mine_ref, pack_ref, other_ref, up_ref, down_ref):
    half, width = up_ref.shape[1:]
    active = joined([mine_ref[0, :, 0:half], other_ref[0, :, 2 * width : 2 * width + half]])
    grad_pre = joined([mine_ref[0, :, half:], other_ref[0, :, 2 * width + half :]])
    x, d = (joined([ref[0, :, i * width : (i + 1) * width] for ref in (pack_ref, other_ref)]) for i in range(2))
    up_ref[0] = dot(grad_pre, x, TN).astype(BF)
    down_ref[0] = dot(active, d, TN).astype(BF)


def weight_pass(mine, pack, other):
    experts, rows, hidden = mine.shape
    width = (pack.shape[2] - hidden) // 2
    return pl.pallas_call(
        weight_kernel,
        grid=(experts,),
        out_shape=[jax.ShapeDtypeStruct((experts, hidden // 2, width), BF)] * 2,
        in_specs=[by_expert(1, rows, n) for n in (hidden, 2 * width, 2 * width + hidden)],
        out_specs=[by_expert(1, hidden // 2, width)] * 2,
        compiler_params=params(),
        cost_estimate=COST,
        name="weight_pass",
    )(mine, pack, other)


def tail_rows(peers):
    return -(-3 * peers // CAP) * CAP


def relay_kernel(peers, select_ref, *refs):
    early_refs, late_refs, out_ref = refs[:peers], refs[peers : 2 * peers], refs[2 * peers]
    slots, tokens = select_ref.shape[1:]
    half, width = slots // 2, out_ref.shape[1]
    total = None
    for m in range(peers):
        term = dot(select_ref[m, 0:half], early_refs[m][half:], TN) + dot(
            select_ref[m, half:], late_refs[m][0:half], TN
        )
        total = term if total is None else total + term
    out_ref[0:tokens] = total.astype(BF)
    tails = [ref[half : half + 3] for ref in late_refs]
    out_ref[tokens:] = joined([*tails, jnp.zeros((tail_rows(peers) - 3 * peers, width), BF)])


def relay_pass(select, early, late):
    peers, slots, tokens = select.shape
    return pl.pallas_call(
        functools.partial(relay_kernel, peers),
        out_shape=jax.ShapeDtypeStruct((tokens + tail_rows(peers), early[0].shape[1]), BF),
        in_specs=[VECTORS] * (1 + 2 * peers),
        out_specs=VECTORS,
        compiler_params=params(),
        cost_estimate=COST,
        name="relay_sum",
    )(select, *early, *late)


def slot_values(tgt, chip, tail, slots):
    at = lax.broadcasted_iota(jnp.int32, (slots, tgt[0].shape[1]), 0) + chip * slots
    column = added(tail).T
    return [jnp.sum(jnp.where(at == t, column, 0.0), axis=0, keepdims=True) for t in tgt]


def targets_in(facts_ref):
    return facts_ref[0:1, :].astype(jnp.int32), facts_ref[1:2, :].astype(jnp.int32)


def near_sum_kernel(me_ref, facts_ref, select_ref, *refs):
    peers, slots, tokens = select_ref.shape
    early_refs, late_refs, (out_ref, gates_ref) = refs[:peers], refs[peers : 2 * peers], refs[2 * peers :]
    half = slots // 2
    tgt = targets_in(facts_ref)
    total, values = None, [jnp.zeros((1, tokens), F32)] * 2
    for m in range(peers):
        term = dot(select_ref[m, 0:half], early_refs[m][0:half], TN) + dot(
            select_ref[m, half:], late_refs[m][0:half], TN
        )
        total = term if total is None else total + term
        more = slot_values(tgt, me_ref[0] ^ m, late_refs[m][half : half + CAP, 0:slots], slots)
        values = [value + new for value, new in zip(values, more)]
    out_ref[...] = total.astype(BF)
    gates_ref[...] = joined(values)


def near_sum(me, facts, select, early, late):
    tokens, width = select.shape[2], early[0].shape[1]
    return pl.pallas_call(
        near_sum_kernel,
        out_shape=[jax.ShapeDtypeStruct((tokens, width), BF), jax.ShapeDtypeStruct((2, tokens), F32)],
        in_specs=[SCALARS] + [VECTORS] * (2 + 2 * len(early)),
        out_specs=[VECTORS] * 2,
        compiler_params=params(),
        cost_estimate=COST,
        name="near_sum",
    )(me, facts, select, *early, *late)


def last_kernel(peers, me_ref, facts_ref, near_ref, values_ref, back_ref, out_ref, gates_ref):
    tokens = near_ref.shape[0]
    slots = EXPERTS // (2 * peers) * CAP
    tgt = targets_in(facts_ref)
    values = [values_ref[k : k + 1, :] for k in range(2)]
    for m in range(peers):
        tail = back_ref[tokens:, 0:slots].astype(F32)[3 * m : 3 * m + 3]
        more = slot_values(tgt, me_ref[0] ^ (peers + m), tail, slots)
        values = [value + new for value, new in zip(values, more)]
    gates_ref[...] = joined(values) / facts_ref[2:4, :]
    out_ref[...] = (near_ref[...].astype(F32) + back_ref[0:tokens].astype(F32)).astype(BF)


def last_pass(peers, me, facts, near, values, back):
    return pl.pallas_call(
        functools.partial(last_kernel, peers),
        out_shape=[jax.ShapeDtypeStruct(near.shape, BF), jax.ShapeDtypeStruct(values.shape, F32)],
        in_specs=[SCALARS] + [VECTORS] * 4,
        out_specs=[VECTORS] * 2,
        compiler_params=params(),
        cost_estimate=COST,
        name="last_sum",
    )(me, facts, near, values, back)


def after(value, *others):
    return lax.optimization_barrier((value, *others))[0]


def per_device(tokens, routes, gate_values, up_weight, down_weight, grad_out):
    chips = lax.axis_size("expert")
    half = chips // 2
    slots = up_weight.shape[0] * CAP
    me = lax.axis_index("expert").astype(jnp.int32).reshape(1)
    core = lax.axis_index("dp").astype(jnp.int32).reshape(1)

    def swap(value, m):
        return lax.ppermute(value, "expert", [(i, i ^ m) for i in range(chips)])

    def swap_core(value):
        return lax.ppermute(value, "dp", [(0, 1), (1, 0)])

    def deal(rows):
        return [rows[0]] + [swap(rows[m], m) for m in range(1, half)]

    g_near, x_near = prepare(routes.T, gate_values.T, grad_out, tokens)
    g_far = swap(g_near, half)
    x_far = swap(tokens, half)
    select, facts, near = rows_pass("near_rows", 1, me, g_near, x_near, half, slots)
    near = deal(near)
    weights = turned(up_weight), turned(down_weight)
    select_far, _, far_first, far_last = rows_pass(
        "far_rows", 2, me, after(g_far, near, weights), x_far, half, slots
    )
    far_first = deal(far_first)
    far_last = deal(after(far_last, far_first[1]))

    gx_first, part, pack, mine = block_pass(0, core, *weights, near, far_first)
    gx_first = deal(gx_first)
    gx_last, pack, mine = block_pass(1, core, *weights, near, far_last, (part, pack, mine))
    relay = relay_pass(select_far, gx_first, deal(gx_last[half:]))
    back = swap(relay, half)
    other = swap_core(after(pack, relay))
    near_last = deal(after(gx_last[:half], relay))

    grad_up, grad_down = weight_pass(mine, pack, other)
    near_tokens, near_gates = near_sum(me, after(facts, grad_up), select, gx_first, near_last)
    grad_tokens, grad_gates = last_pass(half, me, facts, near_tokens, near_gates, after(back, near_tokens))
    return grad_tokens, grad_gates.T, grad_up, grad_down


def solution(mesh):
    placed = (
        P(("group", "expert", "dp"), None),
        P(("group", "expert", "dp"), None),
        P(("group", "expert", "dp"), None),
        P("expert", None, None),
        P("expert", None, None),
        P(("group", "expert", "dp"), None),
    )
    return jax.shard_map(
        per_device,
        mesh=mesh,
        in_specs=placed,
        out_specs=(
            P(("group", "expert", "dp"), None),
            P(("group", "expert", "dp"), None),
            P(("group", "expert"), "dp", None),
            P(("group", "expert"), "dp", None),
        ),
        check_vma=False,
    )
```

```python
import functools

import jax
import jax.numpy as jnp
from jax import lax
from jax.experimental import pallas as pl
from jax.experimental.pallas import tpu as pltpu
from jax.sharding import PartitionSpec as P

EXPERTS = 64
CAP = 16
EIGHTHS = 3
BF = jnp.bfloat16
F32 = jnp.float32
NT = (((1,), (1,)), ((), ()))
NN = (((1,), (0,)), ((), ()))
TN = (((0,), (0,)), ((), ()))


def dot(a, b, dims, precision=None):
    return lax.dot_general(a, b, dims, preferred_element_type=F32, precision=precision)


COST = pl.CostEstimate(flops=1 << 20, bytes_accessed=1 << 20, transcendentals=0)


def params(mebibytes=14):
    return pltpu.CompilerParams(vmem_limit_bytes=mebibytes * 1024 * 1024)


def targets(routes):
    tokens = routes.shape[1]
    first, second = routes[0:1, :], routes[1:2, :]
    experts = lax.broadcasted_iota(jnp.int32, (EXPERTS, tokens), 0)
    one = (experts == first).astype(F32)
    two = (experts == second).astype(F32)
    earlier = lax.broadcasted_iota(jnp.int32, (tokens, tokens), 0) < lax.broadcasted_iota(
        jnp.int32, (tokens, tokens), 1
    )
    before = dot((one + two).astype(BF), earlier.astype(F32).astype(BF), NN)
    rank_one = jnp.sum(one * before, axis=0, keepdims=True).astype(jnp.int32)
    rank_two = jnp.sum(two * (before + one), axis=0, keepdims=True).astype(jnp.int32)
    return first * CAP + rank_one, second * CAP + rank_two


def thirds(value):
    high = value.astype(BF)
    rest = value - high.astype(F32)
    mid = rest.astype(BF)
    return [high, mid, (rest - mid.astype(F32)).astype(BF)]


def added(rows):
    rows = rows.astype(F32)
    return rows[0:1, :] + rows[1:2, :] + rows[2:3, :]


IN_HBM = pl.BlockSpec(memory_space=pltpu.HBM)


def in_hbm(value):
    return pltpu.with_memory_space_constraint(value, pltpu.HBM)


def prepare_kernel(routes_hbm, gates_hbm, g_hbm, x_hbm, out_ref, x_ref, routes_ref, gates_ref, sem):
    tokens, width = g_hbm.shape
    copies = [
        pltpu.make_async_copy(routes_hbm, routes_ref, sem.at[0]),
        pltpu.make_async_copy(gates_hbm, gates_ref, sem.at[1]),
        pltpu.make_async_copy(g_hbm, out_ref.at[0:tokens], sem.at[2]),
        pltpu.make_async_copy(x_hbm, x_ref, sem.at[3]),
    ]
    for copy in copies:
        copy.start()
    out_ref[tokens:, tokens:] = jnp.zeros((CAP, width - tokens), BF)
    copies[0].wait()
    copies[1].wait()
    routes = routes_ref[...].astype(F32).astype(BF)
    gates = gates_ref[...]
    rows = [routes, *thirds(gates[0:1, :]), *thirds(gates[1:2, :]), jnp.zeros((CAP - 8, tokens), BF)]
    out_ref[tokens:, 0:tokens] = jnp.concatenate(rows, axis=0)
    copies[2].wait()
    copies[3].wait()


def prepare(routes, gates, g, x):
    tokens, width = g.shape
    return pl.pallas_call(
        prepare_kernel,
        out_shape=[jax.ShapeDtypeStruct((tokens + CAP, width), BF), jax.ShapeDtypeStruct(x.shape, BF)],
        in_specs=[IN_HBM] * 4,
        out_specs=[pl.BlockSpec(memory_space=pltpu.VMEM)] * 2,
        scratch_shapes=[
            pltpu.VMEM(routes.shape, jnp.int32),
            pltpu.VMEM(gates.shape, F32),
            pltpu.SemaphoreType.DMA((4,)),
        ],
        compiler_params=params(),
        cost_estimate=COST,
        name="prepare",
    )(in_hbm(routes), in_hbm(gates), in_hbm(g), in_hbm(x))


def facts_of(g_ref, tokens):
    facts = g_ref[tokens : tokens + 8, 0:tokens]
    return targets(facts[0:2, :].astype(F32).astype(jnp.int32)), (added(facts[2:5, :]), added(facts[5:8, :]))


def select_slots(targets_of, gates, base, slots):
    rows = lax.broadcasted_iota(jnp.int32, (slots, targets_of[0].shape[1]), 0) + base
    is_one, is_two = rows == targets_of[0], rows == targets_of[1]
    gate = jnp.where(is_one, gates[0], 0.0) + jnp.where(is_two, gates[1], 0.0)
    return jnp.where(is_one | is_two, 1.0, 0.0).astype(BF), jnp.sum(gate, axis=1, keepdims=True)


def whole(*shape):
    return pl.BlockSpec(shape, lambda j: (0,) * len(shape), pipeline_mode=pl.Buffered(1))


def by_expert(*shape):
    return pl.BlockSpec(shape, lambda j: (j,) + (0,) * (len(shape) - 1))


def rows_kernel(peers, sizes, me_ref, g_ref, x_ref, facts_ref, *rows_refs):
    tokens, slots = x_ref.shape[0], sum(sizes)
    tgt, gates = facts_of(g_ref, tokens)
    for m in range(peers):
        select, gate = select_slots(tgt, gates, (me_ref[0] ^ m) * slots, slots)
        x = dot(select, x_ref[...], NN).astype(BF)
        d = (gate * dot(select, g_ref[0:tokens], NN)).astype(BF)
        for i, size in enumerate(sizes):
            at = slice(sum(sizes[:i]), sum(sizes[:i]) + size)
            rows_refs[i * peers + m][0:size] = x[at]
            rows_refs[i * peers + m][size:] = d[at]
    facts_ref[0:2] = jnp.concatenate(tgt, axis=0).astype(F32)
    facts_ref[2:4] = jnp.concatenate(gates, axis=0)
    facts_ref[4:8] = jnp.zeros((4, tokens), F32)


SCALARS = pl.BlockSpec(memory_space=pltpu.SMEM)
VECTORS = pl.BlockSpec(memory_space=pltpu.VMEM)


def rows_pass(name, sizes, me, g, x, peers):
    tokens, width = x.shape
    out = pl.pallas_call(
        functools.partial(rows_kernel, peers, sizes),
        out_shape=[jax.ShapeDtypeStruct((8, tokens), F32)]
        + [jax.ShapeDtypeStruct((2 * size, width), BF) for size in sizes for _ in range(peers)],
        in_specs=[SCALARS] + [VECTORS] * 2,
        out_specs=[VECTORS] * (1 + len(sizes) * peers),
        compiler_params=params(),
        cost_estimate=COST,
        name=name,
    )(me, g, x)
    return out[0], *(list(out[1 + i * peers : 1 + (i + 1) * peers]) for i in range(len(sizes)))


def fetch(weight_hbm, weight_ref, sem, first=0):
    copies = [
        pltpu.make_async_copy(weight_hbm.at[first + j], weight_ref.at[j], sem.at[j])
        for j in range(weight_ref.shape[0])
    ]
    for copy in copies:
        copy.start()
    return copies


def turn_kernel(weight_ref, out_ref):
    out_ref[0] = weight_ref[0].T


def turned(weight):
    experts, hidden, width = weight.shape
    return pl.pallas_call(
        turn_kernel,
        grid=(experts,),
        out_shape=pltpu.HBM((experts, width, hidden), weight.dtype),
        in_specs=[by_expert(1, hidden, width)],
        out_specs=by_expert(1, width, hidden),
        compiler_params=params(),
        cost_estimate=COST,
        name="turned",
    )(in_hbm(weight))


def joined(parts):
    return jnp.concatenate(parts, axis=0)


def of_expert(j, first=0):
    return slice(first + j * CAP, first + (j + 1) * CAP)


def block_kernel(peers, which, core_ref, up_hbm, down_hbm, *refs):
    def take(n):
        nonlocal refs
        taken, refs = refs[:n], refs[n:]
        return taken

    near_refs, far_refs = take(peers), take(peers)
    early_part, _ = (take(1), take(2)) if which else ((), ())
    gx_refs, part_out = take((1 + which) * peers), take(1 - which)
    pack_hbm, mine_hbm, up_ref, down_ref = take(4)
    part_ref = take(1)[0] if which else part_out[0]
    pack_ref, mine_ref, in_sem, out_sem = refs
    experts = up_ref.shape[0]
    width = far_refs[0].shape[1]
    slots, half = experts * CAP, mine_ref.shape[2] // 2
    all_slots = near_refs[0].shape[0] // 2
    start = up_hbm.shape[0] - experts if which else 0
    core = core_ref[0]

    def store(j):
        return (
            pltpu.make_async_copy(pack_ref.at[j], pack_hbm.at[start + j], out_sem.at[j, 0]),
            pltpu.make_async_copy(mine_ref.at[j], mine_hbm.at[start + j], out_sem.at[j, 1]),
        )

    def rows_of(j, kind):
        near, far = kind * all_slots + (start + j) * CAP, kind * slots + j * CAP
        return joined([ref[near : near + CAP] for ref in near_refs] + [ref[far : far + CAP] for ref in far_refs])

    weights = ((up_hbm, up_ref), (down_hbm, down_ref))
    copies = [
        [
            pltpu.make_async_copy(hbm.at[start + j], ref.at[j], in_sem.at[j, i])
            for i, (hbm, ref) in enumerate(weights)
        ]
        for j in range(experts)
    ]
    for group in copies:
        for copy in group:
            copy.start()

    def before(j):
        copies[j][0].wait()
        copies[j][1].wait()
        x, d = rows_of(j, 0), rows_of(j, 1)
        pack_ref[j, :, 0:width] = x
        pack_ref[j, :, width : 2 * width] = d
        return dot(x, up_ref[j], NN), dot(d, down_ref[j], NN)

    following = before(0)
    for j in range(experts):
        pre, h = following
        following = before(j + 1) if j + 1 < experts else None
        sig = 1.0 / (1.0 + jnp.exp(-pre))
        active = (pre * sig).astype(BF)
        grad_pre = (h * sig * (1.0 + pre * (1.0 - sig))).astype(BF)
        gx = dot(grad_pre, up_ref[j], NT).astype(BF)
        prod = active.astype(F32) * h
        part = prod[:, 0:128]
        for i in range(1, prod.shape[1] // 128):
            part = part + prod[:, i * 128 : (i + 1) * 128]
        for m in range(2 * peers):
            mine, to = slice(m * CAP, (m + 1) * CAP), j * CAP
            part_ref[m, to : to + CAP] = part[mine]
            if which:
                gx_refs[m][to : to + CAP] = gx[mine]
            else:
                to = to + m // peers * slots
                gx_refs[m % peers][to : to + CAP] = gx[mine]
        for i, value in enumerate((active, grad_pre)):
            low, high = value[:, 0:half], value[:, half:]
            to = i * half
            mine_ref[j, :, to : to + half] = jnp.where(core == 0, low, high)
            pack_ref[j, :, 2 * width + to : 2 * width + to + half] = jnp.where(core == 0, high, low)
        for out in store(j):
            out.start()
    if which:
        for m in range(2 * peers):
            total = jnp.sum(joined([early_part[0][m], part_ref[m]]).T, axis=0, keepdims=True)
            gx_refs[m][slots:, 0:all_slots] = joined([*thirds(total), jnp.zeros((CAP - 3, all_slots), BF)])
            gx_refs[m][slots:, all_slots:] = jnp.zeros((CAP, width - all_slots), BF)
    for j in range(experts):
        for out in store(j):
            out.wait()


def first_share(experts):
    return max(1, experts * EIGHTHS // 8)


def block_pass(which, core, up, down, near, far, early=()):
    all_experts, width, hidden = up.shape
    experts = first_share(all_experts)
    experts = all_experts - experts if which else experts
    peers = len(near)
    count, slots = 2 * peers * CAP, experts * CAP
    pack, mine, part = (experts, count, 2 * width + hidden), (experts, count, hidden), (2 * peers, slots, 128)
    gx = [(slots + CAP, width)] * (2 * peers) if which else [(2 * slots, width)] * peers
    anywhere = pl.BlockSpec(memory_space=pl.ANY)
    out = pl.pallas_call(
        functools.partial(block_kernel, peers, which),
        out_shape=[jax.ShapeDtypeStruct(shape, BF) for shape in gx]
        + ([] if which else [jax.ShapeDtypeStruct(part, F32)])
        + [jax.ShapeDtypeStruct((all_experts, *shape[1:]), BF) for shape in (pack, mine)],
        in_specs=[SCALARS] + [IN_HBM] * 2 + [VECTORS] * (2 * peers + which) + [anywhere] * (2 * which),
        out_specs=[VECTORS] * (len(gx) + 1 - which) + [anywhere] * 2,
        scratch_shapes=[pltpu.VMEM((experts, width, hidden), BF)] * 2
        + [pltpu.VMEM(part, F32)] * which
        + [
            pltpu.VMEM(pack, BF),
            pltpu.VMEM(mine, BF),
            pltpu.SemaphoreType.DMA((experts, 2)),
            pltpu.SemaphoreType.DMA((experts, 2)),
        ],
        input_output_aliases={4 + 2 * peers + i: len(gx) + i for i in range(2 * which)},
        compiler_params=params(6 * experts + 4),
        cost_estimate=COST,
        name=("first_experts", "last_experts")[which],
    )(core, in_hbm(up), in_hbm(down), *near, *far, *early)
    return list(out[: len(gx)]), *out[len(gx) :]


def weight_kernel(mine_ref, pack_ref, other_ref, up_ref, down_ref):
    half, width = up_ref.shape[1:]
    active = joined([mine_ref[0, :, 0:half], other_ref[0, :, 2 * width : 2 * width + half]])
    grad_pre = joined([mine_ref[0, :, half:], other_ref[0, :, 2 * width + half :]])
    x, d = (joined([ref[0, :, i * width : (i + 1) * width] for ref in (pack_ref, other_ref)]) for i in range(2))
    up_ref[0] = dot(grad_pre, x, TN).astype(BF)
    down_ref[0] = dot(active, d, TN).astype(BF)


def weight_pass(mine, pack, other):
    experts, rows, hidden = mine.shape
    width = (pack.shape[2] - hidden) // 2
    return pl.pallas_call(
        weight_kernel,
        grid=(experts,),
        out_shape=[jax.ShapeDtypeStruct((experts, hidden // 2, width), BF)] * 2,
        in_specs=[by_expert(1, rows, n) for n in (hidden, 2 * width, 2 * width + hidden)],
        out_specs=[by_expert(1, hidden // 2, width)] * 2,
        compiler_params=params(),
        cost_estimate=COST,
        name="weight_pass",
    )(mine, pack, other)


def targets_in(facts_ref):
    return facts_ref[0:1, :].astype(jnp.int32), facts_ref[1:2, :].astype(jnp.int32)


def selection(tgt, base, slots):
    rows = lax.broadcasted_iota(jnp.int32, (slots, tgt[0].shape[1]), 0) + base
    return jnp.where((rows == tgt[0]) | (rows == tgt[1]), 1.0, 0.0).astype(BF)


def tail_rows(peers):
    return -(-3 * peers // CAP) * CAP


def relay_kernel(peers, me_ref, facts_ref, *refs):
    early_refs, late_refs, out_ref = refs[:peers], refs[peers : 2 * peers], refs[2 * peers]
    tokens, width = facts_ref.shape[1], out_ref.shape[1]
    half, rest = early_refs[0].shape[0] // 2, late_refs[0].shape[0] - CAP
    slots = half + rest
    tgt = targets_in(facts_ref)
    total = None
    for m in range(peers):
        rows = joined([early_refs[m][half:], late_refs[m][0:rest]])
        term = dot(selection(tgt, (me_ref[0] ^ m) * slots, slots), rows, TN)
        total = term if total is None else total + term
    out_ref[0:tokens] = total.astype(BF)
    tails = [ref[rest : rest + 3] for ref in late_refs]
    out_ref[tokens:] = joined([*tails, jnp.zeros((tail_rows(peers) - 3 * peers, width), BF)])


def relay_pass(me, facts, early, late):
    peers, tokens = len(early), facts.shape[1]
    return pl.pallas_call(
        functools.partial(relay_kernel, peers),
        out_shape=jax.ShapeDtypeStruct((tokens + tail_rows(peers), early[0].shape[1]), BF),
        in_specs=[SCALARS] + [VECTORS] * (1 + 2 * peers),
        out_specs=VECTORS,
        compiler_params=params(),
        cost_estimate=COST,
        name="relay_sum",
    )(me, facts, *early, *late)


def slot_values(tgt, chip, tail, slots):
    at = lax.broadcasted_iota(jnp.int32, (slots, tgt[0].shape[1]), 0) + chip * slots
    column = added(tail).T
    return [jnp.sum(jnp.where(at == t, column, 0.0), axis=0, keepdims=True) for t in tgt]


def near_sum_kernel(peers, me_ref, facts_ref, *refs):
    early_refs, late_refs, (out_ref, gates_ref) = refs[:peers], refs[peers : 2 * peers], refs[2 * peers :]
    tokens = facts_ref.shape[1]
    half, rest = early_refs[0].shape[0] // 2, late_refs[0].shape[0] - CAP
    slots = half + rest
    tgt = targets_in(facts_ref)
    total, values = None, [jnp.zeros((1, tokens), F32)] * 2
    for m in range(peers):
        rows = joined([early_refs[m][0:half], late_refs[m][0:rest]])
        term = dot(selection(tgt, (me_ref[0] ^ m) * slots, slots), rows, TN)
        total = term if total is None else total + term
        more = slot_values(tgt, me_ref[0] ^ m, late_refs[m][rest : rest + CAP, 0:slots], slots)
        values = [value + new for value, new in zip(values, more)]
    out_ref[...] = total.astype(BF)
    gates_ref[...] = joined(values)


def near_sum(me, facts, early, late):
    tokens, width = facts.shape[1], early[0].shape[1]
    return pl.pallas_call(
        functools.partial(near_sum_kernel, len(early)),
        out_shape=[jax.ShapeDtypeStruct((tokens, width), BF), jax.ShapeDtypeStruct((2, tokens), F32)],
        in_specs=[SCALARS] + [VECTORS] * (1 + 2 * len(early)),
        out_specs=[VECTORS] * 2,
        compiler_params=params(),
        cost_estimate=COST,
        name="near_sum",
    )(me, facts, *early, *late)


def last_kernel(peers, me_ref, facts_ref, near_ref, values_ref, back_ref, out_ref, gates_ref):
    tokens = near_ref.shape[0]
    slots = EXPERTS // (2 * peers) * CAP
    tgt = targets_in(facts_ref)
    values = [values_ref[k : k + 1, :] for k in range(2)]
    for m in range(peers):
        tail = back_ref[tokens:, 0:slots].astype(F32)[3 * m : 3 * m + 3]
        more = slot_values(tgt, me_ref[0] ^ (peers + m), tail, slots)
        values = [value + new for value, new in zip(values, more)]
    gates_ref[...] = joined(values) / facts_ref[2:4, :]
    out_ref[...] = (near_ref[...].astype(F32) + back_ref[0:tokens].astype(F32)).astype(BF)


def last_pass(peers, me, facts, near, values, back):
    return pl.pallas_call(
        functools.partial(last_kernel, peers),
        out_shape=[jax.ShapeDtypeStruct(near.shape, BF), jax.ShapeDtypeStruct(values.shape, F32)],
        in_specs=[SCALARS] + [VECTORS] * 4,
        out_specs=[VECTORS] * 2,
        compiler_params=params(),
        cost_estimate=COST,
        name="last_sum",
    )(me, facts, near, values, back)


def after(value, *others):
    return lax.optimization_barrier((value, *others))[0]


def per_device(tokens, routes, gate_values, up_weight, down_weight, grad_out):
    chips = lax.axis_size("expert")
    half = chips // 2
    slots, first = up_weight.shape[0] * CAP, first_share(up_weight.shape[0]) * CAP
    me = lax.axis_index("expert").astype(jnp.int32).reshape(1)
    core = lax.axis_index("dp").astype(jnp.int32).reshape(1)

    def swap(value, m):
        return lax.ppermute(value, "expert", [(i, i ^ m) for i in range(chips)])

    def swap_core(value):
        return lax.ppermute(value, "dp", [(0, 1), (1, 0)])

    def deal(rows):
        return [rows[0]] + [swap(rows[m], m) for m in range(1, half)]

    g_near, x_near = prepare(routes.T, gate_values.T, grad_out, tokens)
    g_far = swap(g_near, half)
    x_far = swap(tokens, half)
    facts, near = rows_pass("near_rows", (slots,), me, g_near, x_near, half)
    near = deal(near)
    weights = turned(up_weight), turned(down_weight)
    facts_far, far_first, far_last = rows_pass(
        "far_rows", (first, slots - first), me, after(g_far, near, weights), x_far, half
    )
    far_first = deal(far_first)
    far_last = deal(after(far_last, far_first[1]))

    gx_first, part, pack, mine = block_pass(0, core, *weights, near, far_first)
    gx_first = deal(gx_first)
    gx_last, pack, mine = block_pass(1, core, *weights, near, far_last, (part, pack, mine))
    relay = relay_pass(me, facts_far, gx_first, deal(gx_last[half:]))
    back = swap(relay, half)
    other = swap_core(after(pack, relay))
    near_last = deal(after(gx_last[:half], relay))

    grad_up, grad_down = weight_pass(mine, pack, other)
    near_tokens, near_gates = near_sum(me, after(facts, grad_up), gx_first, near_last)
    grad_tokens, grad_gates = last_pass(half, me, facts, near_tokens, near_gates, after(back, near_tokens))
    return grad_tokens, grad_gates.T, grad_up, grad_down


def solution(mesh):
    placed = (
        P(("group", "expert", "dp"), None),
        P(("group", "expert", "dp"), None),
        P(("group", "expert", "dp"), None),
        P("expert", None, None),
        P("expert", None, None),
        P(("group", "expert", "dp"), None),
    )
    return jax.shard_map(
        per_device,
        mesh=mesh,
        in_specs=placed,
        out_specs=(
            P(("group", "expert", "dp"), None),
            P(("group", "expert", "dp"), None),
            P(("group", "expert"), "dp", None),
            P(("group", "expert"), "dp", None),
        ),
        check_vma=False,
    )
```

```python
import functools

import jax
import jax.numpy as jnp
from jax import lax
from jax.experimental import pallas as pl
from jax.experimental.pallas import tpu as pltpu
from jax.sharding import PartitionSpec as P

EXPERTS = 64
CAP = 16
EIGHTHS = 3
BF = jnp.bfloat16
F32 = jnp.float32
NT = (((1,), (1,)), ((), ()))
NN = (((1,), (0,)), ((), ()))
TN = (((0,), (0,)), ((), ()))


def dot(a, b, dims, precision=None):
    return lax.dot_general(a, b, dims, preferred_element_type=F32, precision=precision)


COST = pl.CostEstimate(flops=1 << 20, bytes_accessed=1 << 20, transcendentals=0)


def params(mebibytes=14):
    return pltpu.CompilerParams(vmem_limit_bytes=mebibytes * 1024 * 1024)


def targets(routes):
    tokens = routes.shape[1]
    first, second = routes[0:1, :], routes[1:2, :]
    experts = lax.broadcasted_iota(jnp.int32, (EXPERTS, tokens), 0)
    one = (experts == first).astype(F32)
    two = (experts == second).astype(F32)
    earlier = lax.broadcasted_iota(jnp.int32, (tokens, tokens), 0) < lax.broadcasted_iota(
        jnp.int32, (tokens, tokens), 1
    )
    before = dot((one + two).astype(BF), earlier.astype(F32).astype(BF), NN)
    rank_one = jnp.sum(one * before, axis=0, keepdims=True).astype(jnp.int32)
    rank_two = jnp.sum(two * (before + one), axis=0, keepdims=True).astype(jnp.int32)
    return first * CAP + rank_one, second * CAP + rank_two


def thirds(value):
    high = value.astype(BF)
    rest = value - high.astype(F32)
    mid = rest.astype(BF)
    return [high, mid, (rest - mid.astype(F32)).astype(BF)]


def added(rows):
    rows = rows.astype(F32)
    return rows[0:1, :] + rows[1:2, :] + rows[2:3, :]


IN_HBM = pl.BlockSpec(memory_space=pltpu.HBM)


def in_hbm(value):
    return pltpu.with_memory_space_constraint(value, pltpu.HBM)


def prepare_kernel(routes_hbm, gates_hbm, g_hbm, x_hbm, out_ref, x_ref, routes_ref, gates_ref, sem):
    tokens, width = g_hbm.shape
    copies = [
        pltpu.make_async_copy(routes_hbm, routes_ref, sem.at[0]),
        pltpu.make_async_copy(gates_hbm, gates_ref, sem.at[1]),
        pltpu.make_async_copy(g_hbm, out_ref.at[0:tokens], sem.at[2]),
        pltpu.make_async_copy(x_hbm, x_ref, sem.at[3]),
    ]
    for copy in copies:
        copy.start()
    out_ref[tokens:, tokens:] = jnp.zeros((CAP, width - tokens), BF)
    copies[0].wait()
    copies[1].wait()
    routes = routes_ref[...].astype(F32).astype(BF)
    gates = gates_ref[...]
    rows = [routes, *thirds(gates[0:1, :]), *thirds(gates[1:2, :]), jnp.zeros((CAP - 8, tokens), BF)]
    out_ref[tokens:, 0:tokens] = jnp.concatenate(rows, axis=0)
    copies[2].wait()
    copies[3].wait()


def prepare(routes, gates, g, x):
    tokens, width = g.shape
    return pl.pallas_call(
        prepare_kernel,
        out_shape=[jax.ShapeDtypeStruct((tokens + CAP, width), BF), jax.ShapeDtypeStruct(x.shape, BF)],
        in_specs=[IN_HBM] * 4,
        out_specs=[pl.BlockSpec(memory_space=pltpu.VMEM)] * 2,
        scratch_shapes=[
            pltpu.VMEM(routes.shape, jnp.int32),
            pltpu.VMEM(gates.shape, F32),
            pltpu.SemaphoreType.DMA((4,)),
        ],
        compiler_params=params(),
        cost_estimate=COST,
        name="prepare",
    )(in_hbm(routes), in_hbm(gates), in_hbm(g), in_hbm(x))


def facts_of(g_ref, tokens):
    facts = g_ref[tokens : tokens + 8, 0:tokens]
    return targets(facts[0:2, :].astype(F32).astype(jnp.int32)), (added(facts[2:5, :]), added(facts[5:8, :]))


def select_slots(targets_of, gates, base, slots):
    rows = lax.broadcasted_iota(jnp.int32, (slots, targets_of[0].shape[1]), 0) + base
    is_one, is_two = rows == targets_of[0], rows == targets_of[1]
    gate = jnp.where(is_one, gates[0], 0.0) + jnp.where(is_two, gates[1], 0.0)
    return jnp.where(is_one | is_two, 1.0, 0.0).astype(BF), jnp.sum(gate, axis=1, keepdims=True)


def whole(*shape):
    return pl.BlockSpec(shape, lambda j: (0,) * len(shape), pipeline_mode=pl.Buffered(1))


def by_expert(*shape):
    return pl.BlockSpec(shape, lambda j: (j,) + (0,) * (len(shape) - 1))


def rows_kernel(peers, slots, start, me_ref, g_ref, x_ref, facts_ref, *rows_refs):
    tokens, size = x_ref.shape[0], rows_refs[0].shape[0] // 2
    tgt, gates = facts_of(g_ref, tokens)
    for m in range(peers):
        select, gate = select_slots(tgt, gates, (me_ref[0] ^ m) * slots + start, size)
        rows_refs[m][0:size] = dot(select, x_ref[...], NN).astype(BF)
        rows_refs[m][size:] = (gate * dot(select, g_ref[0:tokens], NN)).astype(BF)
    facts_ref[0:2] = jnp.concatenate(tgt, axis=0).astype(F32)
    facts_ref[2:4] = jnp.concatenate(gates, axis=0)
    facts_ref[4:8] = jnp.zeros((4, tokens), F32)


SCALARS = pl.BlockSpec(memory_space=pltpu.SMEM)
VECTORS = pl.BlockSpec(memory_space=pltpu.VMEM)


def rows_pass(name, slots, start, size, me, g, x, peers):
    tokens, width = x.shape
    out = pl.pallas_call(
        functools.partial(rows_kernel, peers, slots, start),
        out_shape=[jax.ShapeDtypeStruct((8, tokens), F32)] + [jax.ShapeDtypeStruct((2 * size, width), BF)] * peers,
        in_specs=[SCALARS] + [VECTORS] * 2,
        out_specs=[VECTORS] * (1 + peers),
        compiler_params=params(),
        cost_estimate=COST,
        name=name,
    )(me, g, x)
    return out[0], list(out[1:])


def fetch(weight_hbm, weight_ref, sem, first=0):
    copies = [
        pltpu.make_async_copy(weight_hbm.at[first + j], weight_ref.at[j], sem.at[j])
        for j in range(weight_ref.shape[0])
    ]
    for copy in copies:
        copy.start()
    return copies


def turn_kernel(weight_ref, out_ref):
    out_ref[0] = weight_ref[0].T


def turned(weight):
    experts, hidden, width = weight.shape
    return pl.pallas_call(
        turn_kernel,
        grid=(experts,),
        out_shape=pltpu.HBM((experts, width, hidden), weight.dtype),
        in_specs=[by_expert(1, hidden, width)],
        out_specs=by_expert(1, width, hidden),
        compiler_params=params(),
        cost_estimate=COST,
        name="turned",
    )(in_hbm(weight))


def joined(parts):
    return jnp.concatenate(parts, axis=0)


def of_expert(j, first=0):
    return slice(first + j * CAP, first + (j + 1) * CAP)


def block_kernel(peers, which, core_ref, up_hbm, down_hbm, *refs):
    def take(n):
        nonlocal refs
        taken, refs = refs[:n], refs[n:]
        return taken

    near_refs, far_refs = take(peers), take(peers)
    early_part, _ = (take(1), take(2)) if which else ((), ())
    gx_refs, part_out = take((1 + which) * peers), take(1 - which)
    pack_hbm, mine_hbm, up_ref, down_ref = take(4)
    part_ref = take(1)[0] if which else part_out[0]
    pack_ref, mine_ref, in_sem, out_sem = refs
    experts = up_ref.shape[0]
    width = far_refs[0].shape[1]
    slots, half = experts * CAP, mine_ref.shape[2] // 2
    all_slots = near_refs[0].shape[0] // 2
    start = up_hbm.shape[0] - experts if which else 0
    core = core_ref[0]

    def store(j):
        return (
            pltpu.make_async_copy(pack_ref.at[j], pack_hbm.at[start + j], out_sem.at[j, 0]),
            pltpu.make_async_copy(mine_ref.at[j], mine_hbm.at[start + j], out_sem.at[j, 1]),
        )

    def rows_of(j, kind):
        near, far = kind * all_slots + (start + j) * CAP, kind * slots + j * CAP
        return joined([ref[near : near + CAP] for ref in near_refs] + [ref[far : far + CAP] for ref in far_refs])

    weights = ((up_hbm, up_ref), (down_hbm, down_ref))
    copies = [
        [
            pltpu.make_async_copy(hbm.at[start + j], ref.at[j], in_sem.at[j, i])
            for i, (hbm, ref) in enumerate(weights)
        ]
        for j in range(experts)
    ]
    for group in copies:
        for copy in group:
            copy.start()

    def before(j):
        copies[j][0].wait()
        copies[j][1].wait()
        x, d = rows_of(j, 0), rows_of(j, 1)
        pack_ref[j, :, 0:width] = x
        pack_ref[j, :, width : 2 * width] = d
        return dot(x, up_ref[j], NN), dot(d, down_ref[j], NN)

    following = before(0)
    for j in range(experts):
        pre, h = following
        following = before(j + 1) if j + 1 < experts else None
        sig = 1.0 / (1.0 + jnp.exp(-pre))
        active = (pre * sig).astype(BF)
        grad_pre = (h * sig * (1.0 + pre * (1.0 - sig))).astype(BF)
        gx = dot(grad_pre, up_ref[j], NT).astype(BF)
        prod = active.astype(F32) * h
        part = prod[:, 0:128]
        for i in range(1, prod.shape[1] // 128):
            part = part + prod[:, i * 128 : (i + 1) * 128]
        for m in range(2 * peers):
            mine, to = slice(m * CAP, (m + 1) * CAP), j * CAP
            part_ref[m, to : to + CAP] = part[mine]
            if which:
                gx_refs[m][to : to + CAP] = gx[mine]
            else:
                to = to + m // peers * slots
                gx_refs[m % peers][to : to + CAP] = gx[mine]
        for i, value in enumerate((active, grad_pre)):
            low, high = value[:, 0:half], value[:, half:]
            to = i * half
            mine_ref[j, :, to : to + half] = jnp.where(core == 0, low, high)
            pack_ref[j, :, 2 * width + to : 2 * width + to + half] = jnp.where(core == 0, high, low)
        for out in store(j):
            out.start()
    if which:
        for m in range(2 * peers):
            total = jnp.sum(joined([early_part[0][m], part_ref[m]]).T, axis=0, keepdims=True)
            gx_refs[m][slots:, 0:all_slots] = joined([*thirds(total), jnp.zeros((CAP - 3, all_slots), BF)])
            gx_refs[m][slots:, all_slots:] = jnp.zeros((CAP, width - all_slots), BF)
    for j in range(experts):
        for out in store(j):
            out.wait()


def first_share(experts):
    return max(1, experts * EIGHTHS // 8)


def block_pass(which, core, up, down, near, far, early=()):
    all_experts, width, hidden = up.shape
    experts = first_share(all_experts)
    experts = all_experts - experts if which else experts
    peers = len(near)
    count, slots = 2 * peers * CAP, experts * CAP
    pack, mine, part = (experts, count, 2 * width + hidden), (experts, count, hidden), (2 * peers, slots, 128)
    gx = [(slots + CAP, width)] * (2 * peers) if which else [(2 * slots, width)] * peers
    anywhere = pl.BlockSpec(memory_space=pl.ANY)
    out = pl.pallas_call(
        functools.partial(block_kernel, peers, which),
        out_shape=[jax.ShapeDtypeStruct(shape, BF) for shape in gx]
        + ([] if which else [jax.ShapeDtypeStruct(part, F32)])
        + [jax.ShapeDtypeStruct((all_experts, *shape[1:]), BF) for shape in (pack, mine)],
        in_specs=[SCALARS] + [IN_HBM] * 2 + [VECTORS] * (2 * peers + which) + [anywhere] * (2 * which),
        out_specs=[VECTORS] * (len(gx) + 1 - which) + [anywhere] * 2,
        scratch_shapes=[pltpu.VMEM((experts, width, hidden), BF)] * 2
        + [pltpu.VMEM(part, F32)] * which
        + [
            pltpu.VMEM(pack, BF),
            pltpu.VMEM(mine, BF),
            pltpu.SemaphoreType.DMA((experts, 2)),
            pltpu.SemaphoreType.DMA((experts, 2)),
        ],
        input_output_aliases={4 + 2 * peers + i: len(gx) + i for i in range(2 * which)},
        compiler_params=params(6 * experts + 4),
        cost_estimate=COST,
        name=("first_experts", "last_experts")[which],
    )(core, in_hbm(up), in_hbm(down), *near, *far, *early)
    return list(out[: len(gx)]), *out[len(gx) :]


def weight_kernel(mine_ref, pack_ref, other_ref, up_ref, down_ref):
    half, width = up_ref.shape[1:]
    active = joined([mine_ref[0, :, 0:half], other_ref[0, :, 2 * width : 2 * width + half]])
    grad_pre = joined([mine_ref[0, :, half:], other_ref[0, :, 2 * width + half :]])
    x, d = (joined([ref[0, :, i * width : (i + 1) * width] for ref in (pack_ref, other_ref)]) for i in range(2))
    up_ref[0] = dot(grad_pre, x, TN).astype(BF)
    down_ref[0] = dot(active, d, TN).astype(BF)


def weight_pass(mine, pack, other):
    experts, rows, hidden = mine.shape
    width = (pack.shape[2] - hidden) // 2
    return pl.pallas_call(
        weight_kernel,
        grid=(experts,),
        out_shape=[jax.ShapeDtypeStruct((experts, hidden // 2, width), BF)] * 2,
        in_specs=[by_expert(1, rows, n) for n in (hidden, 2 * width, 2 * width + hidden)],
        out_specs=[by_expert(1, hidden // 2, width)] * 2,
        compiler_params=params(),
        cost_estimate=COST,
        name="weight_pass",
    )(mine, pack, other)


def targets_in(facts_ref):
    return facts_ref[0:1, :].astype(jnp.int32), facts_ref[1:2, :].astype(jnp.int32)


def selection(tgt, base, slots):
    rows = lax.broadcasted_iota(jnp.int32, (slots, tgt[0].shape[1]), 0) + base
    return jnp.where((rows == tgt[0]) | (rows == tgt[1]), 1.0, 0.0).astype(BF)


def tail_rows(peers):
    return -(-3 * peers // CAP) * CAP


def relay_kernel(peers, me_ref, facts_ref, *refs):
    early_refs, late_refs, out_ref = refs[:peers], refs[peers : 2 * peers], refs[2 * peers]
    tokens, width = facts_ref.shape[1], out_ref.shape[1]
    half, rest = early_refs[0].shape[0] // 2, late_refs[0].shape[0] - CAP
    slots = half + rest
    tgt = targets_in(facts_ref)
    total = None
    for m in range(peers):
        rows = joined([early_refs[m][half:], late_refs[m][0:rest]])
        term = dot(selection(tgt, (me_ref[0] ^ m) * slots, slots), rows, TN)
        total = term if total is None else total + term
    out_ref[0:tokens] = total.astype(BF)
    tails = [ref[rest : rest + 3] for ref in late_refs]
    out_ref[tokens:] = joined([*tails, jnp.zeros((tail_rows(peers) - 3 * peers, width), BF)])


def relay_pass(me, facts, early, late):
    peers, tokens = len(early), facts.shape[1]
    return pl.pallas_call(
        functools.partial(relay_kernel, peers),
        out_shape=jax.ShapeDtypeStruct((tokens + tail_rows(peers), early[0].shape[1]), BF),
        in_specs=[SCALARS] + [VECTORS] * (1 + 2 * peers),
        out_specs=VECTORS,
        compiler_params=params(),
        cost_estimate=COST,
        name="relay_sum",
    )(me, facts, *early, *late)


def slot_values(tgt, chip, tail, slots):
    at = lax.broadcasted_iota(jnp.int32, (slots, tgt[0].shape[1]), 0) + chip * slots
    column = added(tail).T
    return [jnp.sum(jnp.where(at == t, column, 0.0), axis=0, keepdims=True) for t in tgt]


def near_sum_kernel(peers, me_ref, facts_ref, *refs):
    early_refs, late_refs, (out_ref, gates_ref) = refs[:peers], refs[peers : 2 * peers], refs[2 * peers :]
    tokens = facts_ref.shape[1]
    half, rest = early_refs[0].shape[0] // 2, late_refs[0].shape[0] - CAP
    slots = half + rest
    tgt = targets_in(facts_ref)
    total, values = None, [jnp.zeros((1, tokens), F32)] * 2
    for m in range(peers):
        rows = joined([early_refs[m][0:half], late_refs[m][0:rest]])
        term = dot(selection(tgt, (me_ref[0] ^ m) * slots, slots), rows, TN)
        total = term if total is None else total + term
        more = slot_values(tgt, me_ref[0] ^ m, late_refs[m][rest : rest + CAP, 0:slots], slots)
        values = [value + new for value, new in zip(values, more)]
    out_ref[...] = total.astype(BF)
    gates_ref[...] = joined(values)


def near_sum(me, facts, early, late):
    tokens, width = facts.shape[1], early[0].shape[1]
    return pl.pallas_call(
        functools.partial(near_sum_kernel, len(early)),
        out_shape=[jax.ShapeDtypeStruct((tokens, width), BF), jax.ShapeDtypeStruct((2, tokens), F32)],
        in_specs=[SCALARS] + [VECTORS] * (1 + 2 * len(early)),
        out_specs=[VECTORS] * 2,
        compiler_params=params(),
        cost_estimate=COST,
        name="near_sum",
    )(me, facts, *early, *late)


def last_kernel(peers, me_ref, facts_ref, near_ref, values_ref, back_ref, out_ref, gates_ref):
    tokens = near_ref.shape[0]
    slots = EXPERTS // (2 * peers) * CAP
    tgt = targets_in(facts_ref)
    values = [values_ref[k : k + 1, :] for k in range(2)]
    for m in range(peers):
        tail = back_ref[tokens:, 0:slots].astype(F32)[3 * m : 3 * m + 3]
        more = slot_values(tgt, me_ref[0] ^ (peers + m), tail, slots)
        values = [value + new for value, new in zip(values, more)]
    gates_ref[...] = joined(values) / facts_ref[2:4, :]
    out_ref[...] = (near_ref[...].astype(F32) + back_ref[0:tokens].astype(F32)).astype(BF)


def last_pass(peers, me, facts, near, values, back):
    return pl.pallas_call(
        functools.partial(last_kernel, peers),
        out_shape=[jax.ShapeDtypeStruct(near.shape, BF), jax.ShapeDtypeStruct(values.shape, F32)],
        in_specs=[SCALARS] + [VECTORS] * 4,
        out_specs=[VECTORS] * 2,
        compiler_params=params(),
        cost_estimate=COST,
        name="last_sum",
    )(me, facts, near, values, back)


def after(value, *others):
    return lax.optimization_barrier((value, *others))[0]


def per_device(tokens, routes, gate_values, up_weight, down_weight, grad_out):
    chips = lax.axis_size("expert")
    half = chips // 2
    slots, first = up_weight.shape[0] * CAP, first_share(up_weight.shape[0]) * CAP
    me = lax.axis_index("expert").astype(jnp.int32).reshape(1)
    core = lax.axis_index("dp").astype(jnp.int32).reshape(1)

    def swap(value, m):
        return lax.ppermute(value, "expert", [(i, i ^ m) for i in range(chips)])

    def swap_core(value):
        return lax.ppermute(value, "dp", [(0, 1), (1, 0)])

    def deal(rows):
        return [rows[0]] + [swap(rows[m], m) for m in range(1, half)]

    g_near, x_near = prepare(routes.T, gate_values.T, grad_out, tokens)
    g_far = swap(g_near, half)
    x_far = swap(tokens, half)
    facts, near = rows_pass("near_rows", slots, 0, slots, me, g_near, x_near, half)
    near = deal(near)
    weights = turned(up_weight), turned(down_weight)
    facts_far, far_first = rows_pass("far_first", slots, 0, first, me, after(g_far, near, weights), x_far, half)
    far_first = deal(far_first)
    _, far_last = rows_pass("far_last", slots, first, slots - first, me, after(g_far, far_first[1]), x_far, half)
    far_last = deal(far_last)

    gx_first, part, pack, mine = block_pass(0, core, *weights, near, far_first)
    gx_first = deal(gx_first)
    gx_last, pack, mine = block_pass(1, core, *weights, near, far_last, (part, pack, mine))
    relay = relay_pass(me, facts_far, gx_first, deal(gx_last[half:]))
    back = swap(relay, half)
    other = swap_core(after(pack, relay))
    near_last = deal(after(gx_last[:half], relay))

    grad_up, grad_down = weight_pass(mine, pack, other)
    near_tokens, near_gates = near_sum(me, after(facts, grad_up), gx_first, near_last)
    grad_tokens, grad_gates = last_pass(half, me, facts, near_tokens, near_gates, after(back, near_tokens))
    return grad_tokens, grad_gates.T, grad_up, grad_down


def solution(mesh):
    placed = (
        P(("group", "expert", "dp"), None),
        P(("group", "expert", "dp"), None),
        P(("group", "expert", "dp"), None),
        P("expert", None, None),
        P("expert", None, None),
        P(("group", "expert", "dp"), None),
    )
    return jax.shard_map(
        per_device,
        mesh=mesh,
        in_specs=placed,
        out_specs=(
            P(("group", "expert", "dp"), None),
            P(("group", "expert", "dp"), None),
            P(("group", "expert"), "dp", None),
            P(("group", "expert"), "dp", None),
        ),
        check_vma=False,
    )
```
